32 devices in a mesh: groups: 1, dp: 8 (over z, y), head: 2 (over x), pair: 2 (over core).
Axes of the slice: x: 2, y: 2, z: 4, core: 2. Of those that a mesh axis runs over, the one named last changes fastest.
Arguments:
- queries: bfloat16 [128, 64, 128], P(('groups', 'dp', 'pair'), 'head'), may hold values from -5 to 5
- key_cache: bfloat16 [128, 4, 64, 128], P(('groups', 'dp', 'pair'), 'head'), may hold values from -5 to 5
- value_cache: bfloat16 [128, 4, 64, 128], P(('groups', 'dp', 'pair'), 'head'), may hold values from -6 to 6
- new_key: bfloat16 [128, 4, 128], P(('groups', 'dp', 'pair'), 'head'), may hold values from -5 to 5
- new_value: bfloat16 [128, 4, 128], P(('groups', 'dp', 'pair'), 'head'), may hold values from -6 to 6
- lengths: int32 [128], P(('groups', 'dp', 'pair')), may hold values from 2 to 64, as said below
- expert_input: bfloat16 [128, 4096], P(('groups', 'dp', 'pair')), may hold values from -6 to 6
- routes: int32 [128, 8], P(('groups', 'dp', 'pair')), may hold values from 0 to 15, all different within a row; in each aligned block of 8 rows (0 to 7, 8 to 15, ...) at most 4 rows name the same one
- gate_weights: float32 [128, 8], P(('groups', 'dp', 'pair')), may hold values from 0.05 to 1
- gate_matrix: bfloat16 [16, 768, 4096], P(('dp', 'pair'), 'head'), may hold values from -0.09375 to 0.09375
- up_matrix: bfloat16 [16, 768, 4096], P(('dp', 'pair'), 'head'), may hold values from -0.09375 to 0.09375
- down_matrix: bfloat16 [16, 768, 4096], P(('dp', 'pair'), 'head'), may hold values from -0.21875 to 0.21875
Outputs:
- attention: bfloat16 [128, 64, 128], P(('groups', 'dp', 'pair'), 'head')
- expert_output: bfloat16 [128, 4096], P(('groups', 'dp', 'pair'), 'head')
The draws below stay inside these ranges and needn't reach their ends.
Inputs may be any that keep to these rules, and one draw needn't show every extreme that they name: `routes`: each row names 8 different experts; in each aligned block of 8 rows (the rows of one device) no expert is named by more than 4 rows, and in every draw some block has an expert named by exactly 4 rows. `lengths`: some request has all 64 positions valid.
All inputs are finite; a program needn't handle non-finite values.
Results may differ from the reference program's by a relative error of at most 0.0051.
Values may be sent and summed in bfloat16 or wider, within the bound.
No kernel may reach another device: no remote copies, remote signals or barrier semaphores. Data moves between devices by JAX's collectives and lax.ppermute only.
A program may use at most 64 MiB of HBM per device.

```python
import math
import jax
import jax.numpy as jnp
import numpy as np
from jax import lax

D = 4096
HQ = 64
KVH = 4
HS = 128
EH = 768
TOP = 8
ROW_DEV = 8
L = 64
EXPERTS = 16
ROWS = 128
CAP = 4


def draw_queries(key, part):
    key = jax.random.fold_in(key, 1)
    baseline = jnp.clip(jax.random.normal(key, (ROWS, HQ, HS), jnp.float32), -5.0, 5.0)
    return baseline.astype(jnp.bfloat16)


def draw_key_cache(key, part):
    key = jax.random.fold_in(key, 2)
    baseline = jnp.clip(jax.random.normal(key, (ROWS, KVH, L, HS), jnp.float32), -5.0, 5.0)
    return baseline.astype(jnp.bfloat16)


def draw_lengths(key, part):
    key = jax.random.fold_in(key, 3)
    row_lengths = jax.random.randint(key, (ROWS,), 2, L + 1, jnp.int32)
    longest = jax.random.randint(jax.random.fold_in(key, 4), (), 0, ROWS, jnp.int32)
    return jnp.where(jnp.arange(ROWS) == longest, L, row_lengths).astype(jnp.int32)


def shard_levels(key, shape, pieces, smallest, largest):
    loudness = 1.0
    for dim, blocks in pieces:
        steps = jax.random.uniform(jax.random.fold_in(jax.random.fold_in(key, 6), dim), (blocks,), jnp.float32, smallest / len(pieces), largest / len(pieces))
        loudness = loudness * jnp.repeat(jnp.exp(steps), shape[dim] // blocks).reshape((-1,) + (1,) * (len(shape) - 1 - dim))
    return loudness


def deal_out(stream_key, own, number, rows, amount, top, limit, slope):
    sequence = jax.random.permutation(stream_key, amount)
    heavy_load, usual = portions_of(amount, rows * top, limit, slope, True), portions_of(amount, rows * top, limit, slope, False)
    places = jnp.arange(amount)

    def named(sizes, turn):
        used = int((sizes > 0).sum())
        fixed = max(1, used // 4)
        moved = fixed + (places - fixed + turn * (used - fixed)) % max(1, amount - fixed)
        return jnp.zeros((amount,), jnp.int32).at[sequence[jnp.where(places < fixed, places, moved)]].set(jnp.asarray(sizes, jnp.int32))

    sizes = jnp.where(number % 4 == 0, named(heavy_load, number // 4), named(usual, number - number // 4 - 1))
    mixed = jax.random.permutation(jax.random.fold_in(own, 3), amount)
    giver, sink = mixed[0:amount // 2 * 2:2], mixed[1:amount // 2 * 2:2]
    margin = jnp.minimum(sizes[giver] - 1, limit - sizes[sink]) // 2
    margin = jnp.where((giver == sequence[0]) | (sink == sequence[0]) | (sizes[sink] == 0), 0, jnp.maximum(margin, 0))
    moved = jax.random.randint(jax.random.fold_in(own, 4), (amount // 2,), 0, 1 << 20) % (margin + 1)
    sizes = sizes.at[giver].add(-moved).at[sink].add(moved)
    members = jnp.searchsorted(jnp.cumsum(sizes), jnp.arange(rows * top), side="right").astype(jnp.int32)
    listing = members.reshape(top, rows).T
    listing = listing[jax.random.permutation(jax.random.fold_in(own, 1), rows)]
    turn = jax.random.randint(jax.random.fold_in(own, 2), (rows, 1), 0, top)
    return jnp.take_along_axis(listing, (jnp.arange(top)[None, :] + turn) % top, axis=1)


def portions_of(count, total, bound, slope, full):
    loads = [(1 << 20) // math.isqrt(rank ** slope) + 1 for rank in range(1, count + 1)]
    largest = bound if full else min(bound, max(-(-total // count), total * loads[0] // sum(loads)))
    least = 1 if total - largest >= count - 1 else 0
    holding, spare = [largest] + [least] * (count - 1), total - largest - least * (count - 1)
    while spare > 0:
        movable = [i for i in range(1, count) if holding[i] < largest] or [i for i in range(1, count) if holding[i] < bound]
        mass, left = sum([loads[i] for i in movable]), spare
        for i in movable:
            more = min(bound - holding[i], max(1, left * loads[i] // mass), spare)
            holding[i] = holding[i] + more
            spare = spare - more
    return np.array(holding)


def noise(stream_key, extent, scale, limit, pieces=(), dtype=jnp.bfloat16):
    factor_of = shard_levels(stream_key, extent, pieces, -0.22, 0.18) if pieces else 1.0
    drawn = jax.random.normal(stream_key, extent, jnp.float32) * scale * factor_of
    return jnp.minimum(jnp.maximum(drawn, -limit), limit).astype(dtype)


def setup_inputs(seed: int = 0, part: int = 0) -> dict:
    arg_keys = jax.random.split(jax.random.key(seed), 13)
    part_splits = jax.random.split(jax.random.fold_in(arg_keys[12], part), 13)
    queries = draw_queries(jax.random.fold_in(jax.random.fold_in(arg_keys[12], part), 71), part)
    key_cache = draw_key_cache(jax.random.fold_in(jax.random.fold_in(arg_keys[12], part), 71), part)
    value_cache = noise(part_splits[2], (ROWS, KVH, L, HS), 1.0, 6.0, ((0, 16), (1, 2)))
    new_key = noise(part_splits[3], (ROWS, KVH, HS), 1.0, 5.0, ((0, 16), (1, 2)))
    new_value = noise(part_splits[4], (ROWS, KVH, HS), 1.0, 6.0, ((0, 16), (1, 2)))
    lengths = draw_lengths(jax.random.fold_in(jax.random.fold_in(arg_keys[12], part), 71), part)
    expert_input = noise(part_splits[6], (ROWS, D), 1.0, 6.0, ((0, 16),))
    routes_keys = jax.random.split(jax.random.fold_in(part_splits[7], 1), ROWS // ROW_DEV)
    routes_turns = jax.random.permutation(jax.random.fold_in(part_splits[7], 3), ROWS // ROW_DEV)
    routes = jax.vmap(lambda own, number: deal_out(jax.random.fold_in(part_splits[7], 2), own, number, ROW_DEV, EXPERTS, TOP, CAP, 2))(routes_keys, routes_turns).reshape((ROWS, TOP))
    gate_weights = jnp.clip(jnp.exp(math.log(1.0) - 2.9957323 * jax.random.uniform(part_splits[8], (ROWS, TOP), jnp.float32) ** shard_levels(part_splits[8], (ROWS, TOP), ((0, 16),), -0.2, 0.2)), 0.05, 1.0)
    gate_matrix = noise(arg_keys[9], (EXPERTS, EH, D), D ** -0.5, 0.09375, ((0, 16), (1, 2)))
    up_matrix = noise(arg_keys[10], (EXPERTS, EH, D), D ** -0.5, 0.09375, ((0, 16), (1, 2)))
    down_matrix = noise(arg_keys[11], (EXPERTS, EH, D), EH ** -0.5, 0.21875, ((0, 16), (1, 2)))
    return {"queries": queries, "key_cache": key_cache, "value_cache": value_cache, "new_key": new_key, "new_value": new_value, "lengths": lengths, "expert_input": expert_input, "routes": routes, "gate_weights": gate_weights, "gate_matrix": gate_matrix, "up_matrix": up_matrix, "down_matrix": down_matrix}


def attend(queries, key_cache, value_cache, new_key, new_value, lengths):
    grouping = HQ // KVH
    scaling = HS ** -0.5
    query_float = queries.astype(jnp.float32).reshape(ROWS, KVH, grouping, HS)
    scores = jnp.einsum("rgqd,rgld->rgql", query_float, key_cache.astype(jnp.float32)) * scaling
    fresh_score = jnp.einsum("rgqd,rgd->rgq", query_float, new_key.astype(jnp.float32)) * scaling
    valid_mask = (jnp.arange(L)[None, :] < lengths[:, None])[:, None, None, :]
    masked = jnp.where(valid_mask, scores, jnp.float32(-1e30))
    highest = jnp.maximum(jnp.max(masked, axis=-1), fresh_score)
    weights = jnp.where(valid_mask, jnp.exp(masked - highest[..., None]), jnp.float32(0.0))
    fresh_weight = jnp.exp(fresh_score - highest)
    totals = jnp.sum(weights, axis=-1) + fresh_weight
    rounded = lax.optimization_barrier(weights.astype(jnp.bfloat16)).astype(jnp.float32)
    fresh_rounded = lax.optimization_barrier(fresh_weight.astype(jnp.bfloat16)).astype(jnp.float32)
    accumulated = jnp.einsum("rgql,rgld->rgqd", rounded, value_cache.astype(jnp.float32))
    accumulated = accumulated + fresh_rounded[..., None] * new_value.astype(jnp.float32)[:, :, None, :]
    return (accumulated / totals[..., None]).reshape(ROWS, HQ, HS).astype(jnp.bfloat16)


def reference(queries, key_cache, value_cache, new_key, new_value, lengths, expert_input, routes, gate_weights, gate_matrix, up_matrix, down_matrix):
    attention = attend(queries, key_cache, value_cache, new_key, new_value, lengths)
    input_float = expert_input.astype(jnp.float32)
    coefficient = jnp.sum(jnp.where(routes[:, :, None] == jnp.arange(EXPERTS)[None, None, :], gate_weights[:, :, None], 0.0), axis=1)
    row_limit = min(EXPERTS * CAP, ROWS)
    highest_precision = lax.Precision.HIGHEST

    def one_expert(running, expert_id):
        member = jnp.any(routes == expert_id, axis=1)
        order_key = jnp.where(member, 0, ROWS) + jnp.arange(ROWS)
        chosen = jnp.argsort(order_key)[:row_limit]
        picked_rows = input_float[chosen]
        route_weight = coefficient[chosen, expert_id]
        gate_part = jnp.dot(picked_rows, gate_matrix[expert_id].astype(jnp.float32).T, precision=highest_precision)
        up_part = jnp.dot(picked_rows, up_matrix[expert_id].astype(jnp.float32).T, precision=highest_precision)
        hidden = lax.optimization_barrier((jax.nn.silu(gate_part) * up_part).astype(jnp.bfloat16)).astype(jnp.float32)
        result = jnp.dot(hidden, down_matrix[expert_id].astype(jnp.float32), precision=highest_precision)
        return running.at[chosen].add(route_weight[:, None] * result), None

    summed, unused = lax.scan(one_expert, jnp.zeros((ROWS, D), jnp.float32), jnp.arange(EXPERTS))
    return attention, summed.astype(jnp.bfloat16)
```

```python
import functools

import jax
import jax.numpy as jnp
from jax import lax
from jax.experimental import pallas as pl
from jax.experimental.pallas import tpu as pltpu
from jax.sharding import PartitionSpec as P

LANES = 128
BF16 = jnp.bfloat16
F32 = jnp.float32


def attend_local(queries, key_cache, value_cache, new_key, new_value, lengths):
    row_count, head_count, head_size = queries.shape
    kv_heads = key_cache.shape[1]
    cache_len = key_cache.shape[2]
    grouping = head_count // kv_heads
    scaling = head_size ** (-0.5)
    grouped = queries.reshape(row_count, kv_heads, grouping, head_size)
    scores = (
        jnp.einsum("rgqd,rgld->rgql", grouped, key_cache, preferred_element_type=jnp.float32)
        * scaling
    )
    fresh_score = (
        jnp.einsum("rgqd,rgd->rgq", grouped, new_key, preferred_element_type=jnp.float32) * scaling
    )
    valid_mask = (jnp.arange(cache_len)[None, :] < lengths[:, None])[:, None, None, :]
    masked = jnp.where(valid_mask, scores, jnp.float32(-1e30))
    highest = jnp.maximum(jnp.max(masked, axis=-1), fresh_score)
    weights = jnp.where(valid_mask, jnp.exp(masked - highest[..., None]), jnp.float32(0.0))
    fresh_weight = jnp.exp(fresh_score - highest)
    totals = jnp.sum(weights, axis=-1) + fresh_weight
    accumulated = jnp.einsum(
        "rgql,rgld->rgqd",
        weights.astype(jnp.bfloat16),
        value_cache,
        preferred_element_type=jnp.float32,
    )
    accumulated = accumulated + jnp.einsum(
        "rgq,rgd->rgqd",
        fresh_weight.astype(jnp.bfloat16),
        new_value,
        preferred_element_type=jnp.float32,
    )
    return (
        (accumulated / totals[..., None])
        .reshape(row_count, head_count, head_size)
        .astype(jnp.bfloat16)
    )


def partner(index, step, count):
    if count & (count - 1) == 0:
        return index ^ step
    return (index + step) % count


def home_of(index, step, count):
    if count & (count - 1) == 0:
        return index ^ step
    return (index - step + count) % count


def ffn_kernel(dims, expert_ref, base_ref, own_ref, other_ref, gate_hbm, up_hbm, down_hbm, out_ref,
               gate, up, down, gate_sems, up_sems, down_sems):
    dev_rows, width, route_count, capacity, heads, sources = dims
    hidden_size = gate.shape[0]
    chunks = gate_sems.shape[0]
    chunk = hidden_size // chunks
    share = width // heads
    copies = []
    for i in range(chunks):
        part = pl.ds(i * chunk, chunk)
        a = pltpu.make_async_copy(gate_hbm.at[0, part], gate.at[part], gate_sems.at[i])
        b = pltpu.make_async_copy(up_hbm.at[0, part], up.at[part], up_sems.at[i])
        a.start()
        b.start()
        copies.append((a, b))
    down_copies = []
    for h in range(heads):
        part = pl.ds(h * share, share)
        a = pltpu.make_async_copy(down_hbm.at[0, :, part], down.at[:, part], down_sems.at[h])
        a.start()
        down_copies.append(a)

    rows = sources * dev_rows
    slots = sources * capacity
    names = jnp.concatenate([own_ref[:, width:], other_ref[:, width:]], axis=0)
    lane = lax.broadcasted_iota(jnp.int32, names.shape, 1)
    expert = expert_ref[0].astype(F32)
    named = jnp.where((lane < route_count) & (names.astype(F32) == expert), 1.0, 0.0).astype(BF16)
    member = lax.dot_general(
        jnp.ones((8, names.shape[1]), BF16), named, (((1,), (1,)), ((), ())),
        preferred_element_type=F32,
    )
    above = lax.broadcasted_iota(jnp.int32, (rows, rows), 0)
    below = lax.broadcasted_iota(jnp.int32, (rows, rows), 1)
    earlier = (above < below) & (above // dev_rows == below // dev_rows)
    rank = jnp.dot(
        member.astype(BF16), jnp.where(earlier, 1.0, 0.0).astype(BF16), preferred_element_type=F32
    )
    target = jnp.where(member > 0.5, base_ref[...] + rank.astype(jnp.int32), -1)
    slot = lax.broadcasted_iota(jnp.int32, (slots, rows), 0)
    placing = jnp.where(slot == target[0:1], 1.0, 0.0).astype(BF16)

    inputs = jnp.concatenate([own_ref[:, :width], other_ref[:, :width]], axis=0)
    contract = (((1,), (1,)), ((), ()))
    parts = []
    for i in range(chunks):
        copies[i][0].wait()
        copies[i][1].wait()
        part = pl.ds(i * chunk, chunk)
        gate_part = lax.dot_general(inputs, gate[part], contract, preferred_element_type=F32)
        up_part = lax.dot_general(inputs, up[part], contract, preferred_element_type=F32)
        hidden = (gate_part / (1.0 + jnp.exp(-gate_part)) * up_part).astype(BF16)
        parts.append(jnp.dot(placing, hidden, preferred_element_type=F32).astype(BF16))
    hidden = jnp.concatenate(parts, axis=1)

    pieces = 8 // capacity
    piece = share // pieces
    row = lax.broadcasted_iota(jnp.int32, (8, piece), 0)
    for h in range(heads):
        down_copies[h].wait()
        result = jnp.dot(hidden, down[:, h * share : (h + 1) * share], preferred_element_type=F32)
        for block in range(slots // 8):
            columns = [
                result[block * 8 : block * 8 + 8, k * piece : (k + 1) * piece]
                for k in range(pieces)
            ]
            for j in range(pieces):
                packed = None
                for k in range(pieces):
                    shift = (k - j) * capacity % 8
                    moved = pltpu.roll(columns[k], shift, 0) if shift else columns[k]
                    packed = moved if packed is None else jnp.where(row // capacity == k, moved, packed)
                out_ref[(block * pieces + j) * heads + h] = packed.astype(BF16)


def expert_block(expert, base, own, other, gate_matrix, up_matrix, down_matrix, dims):
    dev_rows, width, route_count, capacity, heads, sources = dims
    hidden_size = gate_matrix.shape[1]
    chunks = max(1, hidden_size // 128)
    while hidden_size % chunks:
        chunks -= 1
    piece = width // heads * capacity // 8
    return pl.pallas_call(
        functools.partial(ffn_kernel, dims),
        out_shape=jax.ShapeDtypeStruct((sources * heads, 8, piece), BF16),
        in_specs=[
            pl.BlockSpec(memory_space=pltpu.SMEM),
            pl.BlockSpec(memory_space=pltpu.VMEM),
            pl.BlockSpec(memory_space=pltpu.VMEM),
            pl.BlockSpec(memory_space=pltpu.VMEM),
            pl.BlockSpec(memory_space=pl.ANY),
            pl.BlockSpec(memory_space=pl.ANY),
            pl.BlockSpec(memory_space=pl.ANY),
        ],
        out_specs=pl.BlockSpec(memory_space=pltpu.VMEM),
        scratch_shapes=[
            pltpu.VMEM((hidden_size, width), BF16),
            pltpu.VMEM((hidden_size, width), BF16),
            pltpu.VMEM((hidden_size, width), BF16),
            pltpu.SemaphoreType.DMA((chunks,)),
            pltpu.SemaphoreType.DMA((chunks,)),
            pltpu.SemaphoreType.DMA((heads,)),
        ],
        compiler_params=pltpu.CompilerParams(vmem_limit_bytes=40 * 1024 * 1024),
        cost_estimate=pl.CostEstimate(
            flops=2 * sources * dev_rows * width * hidden_size * 3,
            bytes_accessed=hidden_size * width * 6,
            transcendentals=sources * dev_rows * hidden_size,
        ),
    )(expert, base, own, other, gate_matrix, up_matrix, down_matrix)


def combine_kernel(pieces, terms, lhs_ref, got_ref, out_ref):
    blocks, rows, piece = got_ref.shape
    got = got_ref[...].reshape(blocks * rows, piece)
    sums = jnp.dot(lhs_ref[...], got, preferred_element_type=F32)
    height = out_ref.shape[0]
    for k in range(pieces):
        total = None
        for t in range(terms):
            start = (k * terms + t) * height
            term = sums[start : start + height]
            total = term if total is None else total + term
        out_ref[:, k * piece : (k + 1) * piece] = total.astype(BF16)


def body(
    queries,
    key_cache,
    value_cache,
    new_key,
    new_value,
    lengths,
    expert_input,
    routes,
    gate_weights,
    gate_matrix,
    up_matrix,
    down_matrix,
):
    dev_rows, route_count = routes.shape
    width = expert_input.shape[1]
    steps, pairs, heads = lax.axis_size("dp"), lax.axis_size("pair"), lax.axis_size("head")
    sources = steps * pairs
    capacity = max(2, dev_rows * route_count // sources)
    my_dp, my_pair = lax.axis_index("dp"), lax.axis_index("pair")

    labels = jnp.pad(routes.astype(BF16), ((0, 0), (0, LANES - route_count)))
    block = jnp.concatenate([expert_input, labels], axis=1)
    order = sorted(range(1, steps), key=lambda s: (-(s // 4), -(s // 2), s))
    arrived = [block]
    for step in order:
        pairs_of = [(i, partner(i, step, steps)) for i in range(steps)]
        arrived.append(lax.ppermute(block, "dp", pairs_of))
    own = jnp.concatenate(arrived, axis=0)
    other = lax.ppermute(own, "pair", [(0, 1), (1, 0)])
    homes = jnp.stack([home_of(my_dp, step, steps) for step in [0] + order])
    homes = jnp.stack([homes * pairs + my_pair, homes * pairs + (1 - my_pair)])
    base = jnp.broadcast_to(homes[:, :, None] * capacity, homes.shape + (dev_rows,))
    base = jnp.broadcast_to(base.reshape(1, -1).astype(jnp.int32), (8, sources * dev_rows))
    expert = (my_dp * pairs + my_pair).astype(jnp.int32).reshape(1)

    dims = (dev_rows, width, route_count, capacity, heads, sources)
    sent = expert_block(expert, base, own, other, gate_matrix, up_matrix, down_matrix, dims)
    got = lax.all_to_all(sent, ("dp", "pair", "head"), split_axis=0, concat_axis=0, tiled=True)

    attention = attend_local(queries, key_cache, value_cache, new_key, new_value, lengths)

    named = routes[:, :, None] == jnp.arange(sources)[None, None, :]
    member = jnp.any(named, axis=1)
    coefficient = jnp.sum(jnp.where(named, gate_weights[:, :, None], 0.0), axis=1)
    slot = jnp.cumsum(member.astype(jnp.int32), axis=0) - 1
    pieces = 8 // capacity
    terms = []
    rest = coefficient
    for _ in range(3):
        term = lax.reduce_precision(rest, 8, 7)
        terms.append(term)
        rest = rest - term
    terms = jnp.stack(terms)
    place = jnp.arange(8)
    hit = (
        (place[None, None, None, :] // capacity == jnp.arange(pieces)[:, None, None, None])
        & (place[None, None, None, :] % capacity == slot[None, :, :, None])
        & member[None, :, :, None]
    )
    lhs = jnp.where(hit[:, None], terms[None, :, :, :, None], 0.0)
    lhs = jnp.broadcast_to(lhs[:, :, :, :, None, :], lhs.shape[:4] + (heads, 8))
    lhs = lhs.reshape(pieces * 3 * dev_rows, sources * heads * 8).astype(BF16)
    expert_output = pl.pallas_call(
        functools.partial(combine_kernel, pieces, 3),
        out_shape=jax.ShapeDtypeStruct((dev_rows, width // heads), BF16),
    )(lhs, got)
    return (attention, expert_output)


def solution(mesh):
    placed = (
        P(("groups", "dp", "pair"), "head", None),
        P(("groups", "dp", "pair"), "head", None, None),
        P(("groups", "dp", "pair"), "head", None, None),
        P(("groups", "dp", "pair"), "head", None),
        P(("groups", "dp", "pair"), "head", None),
        P(("groups", "dp", "pair")),
        P(("groups", "dp", "pair"), None),
        P(("groups", "dp", "pair"), None),
        P(("groups", "dp", "pair"), None),
        P(("dp", "pair"), "head", None),
        P(("dp", "pair"), "head", None),
        P(("dp", "pair"), "head", None),
    )
    return jax.shard_map(
        body,
        mesh=mesh,
        in_specs=placed,
        out_specs=(P(("groups", "dp", "pair"), "head", None), P(("groups", "dp", "pair"), "head")),
        check_vma=False,
    )
```

```python
import functools

import jax
import jax.numpy as jnp
from jax import lax
from jax.experimental import pallas as pl
from jax.experimental.pallas import tpu as pltpu
from jax.sharding import PartitionSpec as P

BF16 = jnp.bfloat16
F32 = jnp.float32


def attend_local(queries, key_cache, value_cache, new_key, new_value, lengths):
    row_count, head_count, head_size = queries.shape
    kv_heads = key_cache.shape[1]
    cache_len = key_cache.shape[2]
    grouping = head_count // kv_heads
    scaling = head_size ** (-0.5)
    grouped = queries.reshape(row_count, kv_heads, grouping, head_size)
    scores = (
        jnp.einsum("rgqd,rgld->rgql", grouped, key_cache, preferred_element_type=jnp.float32)
        * scaling
    )
    fresh_score = (
        jnp.einsum("rgqd,rgd->rgq", grouped, new_key, preferred_element_type=jnp.float32) * scaling
    )
    valid_mask = (jnp.arange(cache_len)[None, :] < lengths[:, None])[:, None, None, :]
    masked = jnp.where(valid_mask, scores, jnp.float32(-1e30))
    highest = jnp.maximum(jnp.max(masked, axis=-1), fresh_score)
    weights = jnp.where(valid_mask, jnp.exp(masked - highest[..., None]), jnp.float32(0.0))
    fresh_weight = jnp.exp(fresh_score - highest)
    totals = jnp.sum(weights, axis=-1) + fresh_weight
    accumulated = jnp.einsum(
        "rgql,rgld->rgqd",
        weights.astype(jnp.bfloat16),
        value_cache,
        preferred_element_type=jnp.float32,
    )
    accumulated = accumulated + jnp.einsum(
        "rgq,rgd->rgqd",
        fresh_weight.astype(jnp.bfloat16),
        new_value,
        preferred_element_type=jnp.float32,
    )
    return (
        (accumulated / totals[..., None])
        .reshape(row_count, head_count, head_size)
        .astype(jnp.bfloat16)
    )


def dispatch_kernel(capacity, routes_ref, rows_ref, out_ref):
    dev_rows, route_count = routes_ref.shape
    total, piece = out_ref.shape
    pieces = 8 // capacity
    target = lax.broadcasted_iota(jnp.int32, (dev_rows, total), 1)
    named = jnp.zeros((dev_rows, total), jnp.bool_)
    for j in range(route_count):
        named = named | (routes_ref[:, j : j + 1] == target // 8)
    member = jnp.where(named, 1.0, 0.0)
    above = lax.broadcasted_iota(jnp.int32, (dev_rows, dev_rows), 0)
    below = lax.broadcasted_iota(jnp.int32, (dev_rows, dev_rows), 1)
    earlier = jnp.where(below < above, 1.0, 0.0).astype(BF16)
    rank = jnp.dot(earlier, member.astype(BF16), preferred_element_type=F32)
    taken = jnp.where(rank == (target % capacity).astype(F32), member, 0.0)
    cut = target % 8 // capacity
    placing = jnp.concatenate(
        [jnp.where(cut == k, taken, 0.0) for k in range(pieces)], axis=0
    ).astype(BF16)
    rows = jnp.concatenate(
        [rows_ref[:, k * piece : (k + 1) * piece] for k in range(pieces)], axis=0
    )
    contract = (((0,), (0,)), ((), ()))
    out_ref[...] = lax.dot_general(
        placing, rows, contract, preferred_element_type=F32
    ).astype(BF16)


def ffn_kernel(dims, got_ref, gate_hbm, up_hbm, down_hbm, out_ref,
               gate, up, down, gate_sems, up_sems, down_sems):
    capacity, heads, sources = dims
    hidden_size, width = gate.shape
    chunks = gate_sems.shape[0]
    chunk = hidden_size // chunks
    share = width // heads
    pieces = 8 // capacity
    copies = []
    for i in range(chunks):
        part = pl.ds(i * chunk, chunk)
        a = pltpu.make_async_copy(gate_hbm.at[0, part], gate.at[part], gate_sems.at[i])
        b = pltpu.make_async_copy(up_hbm.at[0, part], up.at[part], up_sems.at[i])
        a.start()
        b.start()
        copies.append((a, b))
    down_copies = []
    for h in range(heads):
        part = pl.ds(h * share, share)
        a = pltpu.make_async_copy(down_hbm.at[0, :, part], down.at[:, part], down_sems.at[h])
        a.start()
        down_copies.append(a)

    rows = got_ref[...]
    total, piece = rows.shape
    contract = (((1,), (1,)), ((), ()))

    def project(matrix, part):
        terms = [
            lax.dot_general(
                rows, matrix[part, k * piece : (k + 1) * piece], contract,
                preferred_element_type=F32,
            )
            for k in range(pieces)
        ]
        cut = lax.broadcasted_iota(jnp.int32, terms[0].shape, 0) % 8 // capacity
        result = None
        for j in range(pieces):
            summed = None
            for k in range(pieces):
                shift = (j - k) * capacity % total
                moved = pltpu.roll(terms[k], shift, 0) if shift else terms[k]
                summed = moved if summed is None else summed + moved
            result = summed if result is None else jnp.where(cut == j, summed, result)
        return result

    parts = []
    for i in range(chunks):
        part = pl.ds(i * chunk, chunk)
        copies[i][0].wait()
        gate_part = project(gate, part)
        copies[i][1].wait()
        up_part = project(up, part)
        parts.append((gate_part / (1.0 + jnp.exp(-gate_part)) * up_part).astype(BF16))
    hidden = jnp.concatenate(parts, axis=1)

    width_out = share // pieces
    cut = lax.broadcasted_iota(jnp.int32, (total, width_out), 0) % 8 // capacity
    for h in range(heads):
        down_copies[h].wait()
        packed = None
        for k in range(pieces):
            start = h * share + k * width_out
            result = jnp.dot(
                hidden, down[:, start : start + width_out], preferred_element_type=F32
            )
            packed = result if packed is None else jnp.where(cut == k, result, packed)
        packed = packed.astype(BF16)
        for q in range(sources):
            out_ref[q * heads + h] = packed[q * 8 : q * 8 + 8]


def expert_block(got, gate_matrix, up_matrix, down_matrix, capacity, heads):
    sources = got.shape[0]
    hidden_size, width = gate_matrix.shape[1:]
    chunks = max(1, hidden_size // 128)
    while hidden_size % chunks:
        chunks -= 1
    piece = width // heads * capacity // 8
    return pl.pallas_call(
        functools.partial(ffn_kernel, (capacity, heads, sources)),
        out_shape=jax.ShapeDtypeStruct((sources * heads, 8, piece), BF16),
        in_specs=[
            pl.BlockSpec(memory_space=pltpu.VMEM),
            pl.BlockSpec(memory_space=pl.ANY),
            pl.BlockSpec(memory_space=pl.ANY),
            pl.BlockSpec(memory_space=pl.ANY),
        ],
        out_specs=pl.BlockSpec(memory_space=pltpu.VMEM),
        scratch_shapes=[
            pltpu.VMEM((hidden_size, width), BF16),
            pltpu.VMEM((hidden_size, width), BF16),
            pltpu.VMEM((hidden_size, width), BF16),
            pltpu.SemaphoreType.DMA((chunks,)),
            pltpu.SemaphoreType.DMA((chunks,)),
            pltpu.SemaphoreType.DMA((heads,)),
        ],
        compiler_params=pltpu.CompilerParams(vmem_limit_bytes=58 * 1024 * 1024),
        cost_estimate=pl.CostEstimate(
            flops=2 * sources * 8 * width * hidden_size * 3,
            bytes_accessed=hidden_size * width * 6,
            transcendentals=sources * 8 * hidden_size,
        ),
    )(got.reshape(sources * 8, -1), gate_matrix, up_matrix, down_matrix)


def combine_kernel(pieces, terms, lhs_ref, got_ref, out_ref):
    blocks, rows, piece = got_ref.shape
    got = got_ref[...].reshape(blocks * rows, piece)
    sums = jnp.dot(lhs_ref[...], got, preferred_element_type=F32)
    height = out_ref.shape[0]
    for k in range(pieces):
        total = None
        for t in range(terms):
            start = (k * terms + t) * height
            term = sums[start : start + height]
            total = term if total is None else total + term
        out_ref[:, k * piece : (k + 1) * piece] = total.astype(BF16)


def body(
    queries,
    key_cache,
    value_cache,
    new_key,
    new_value,
    lengths,
    expert_input,
    routes,
    gate_weights,
    gate_matrix,
    up_matrix,
    down_matrix,
):
    dev_rows, route_count = routes.shape
    width = expert_input.shape[1]
    steps, pairs, heads = lax.axis_size("dp"), lax.axis_size("pair"), lax.axis_size("head")
    sources = steps * pairs
    capacity = max(2, dev_rows * route_count // sources)
    pieces = 8 // capacity

    outgoing = pl.pallas_call(
        functools.partial(dispatch_kernel, capacity),
        out_shape=jax.ShapeDtypeStruct((sources * 8, width // pieces), BF16),
        compiler_params=pltpu.CompilerParams(vmem_limit_bytes=8 * 1024 * 1024),
    )(routes, expert_input)
    arrived = lax.all_to_all(
        outgoing.reshape(sources, 8, -1), ("dp", "pair"), split_axis=0, concat_axis=0, tiled=True
    )
    sent = expert_block(arrived, gate_matrix, up_matrix, down_matrix, capacity, heads)
    got = lax.all_to_all(sent, ("dp", "pair", "head"), split_axis=0, concat_axis=0, tiled=True)

    attention = attend_local(queries, key_cache, value_cache, new_key, new_value, lengths)

    named = routes[:, :, None] == jnp.arange(sources)[None, None, :]
    member = jnp.any(named, axis=1)
    coefficient = jnp.sum(jnp.where(named, gate_weights[:, :, None], 0.0), axis=1)
    slot = jnp.cumsum(member.astype(jnp.int32), axis=0) - 1
    terms = []
    rest = coefficient
    for _ in range(3):
        term = lax.reduce_precision(rest, 8, 7)
        terms.append(term)
        rest = rest - term
    terms = jnp.stack(terms)
    place = jnp.arange(8)
    hit = (
        (place[None, None, None, :] // capacity == jnp.arange(pieces)[:, None, None, None])
        & (place[None, None, None, :] % capacity == slot[None, :, :, None])
        & member[None, :, :, None]
    )
    lhs = jnp.where(hit[:, None], terms[None, :, :, :, None], 0.0)
    lhs = jnp.broadcast_to(lhs[:, :, :, :, None, :], lhs.shape[:4] + (heads, 8))
    lhs = lhs.reshape(pieces * 3 * dev_rows, sources * heads * 8).astype(BF16)
    expert_output = pl.pallas_call(
        functools.partial(combine_kernel, pieces, 3),
        out_shape=jax.ShapeDtypeStruct((dev_rows, width // heads), BF16),
        compiler_params=pltpu.CompilerParams(vmem_limit_bytes=8 * 1024 * 1024),
    )(lhs, got)
    return (attention, expert_output)


def solution(mesh):
    placed = (
        P(("groups", "dp", "pair"), "head", None),
        P(("groups", "dp", "pair"), "head", None, None),
        P(("groups", "dp", "pair"), "head", None, None),
        P(("groups", "dp", "pair"), "head", None),
        P(("groups", "dp", "pair"), "head", None),
        P(("groups", "dp", "pair")),
        P(("groups", "dp", "pair"), None),
        P(("groups", "dp", "pair"), None),
        P(("groups", "dp", "pair"), None),
        P(("dp", "pair"), "head", None),
        P(("dp", "pair"), "head", None),
        P(("dp", "pair"), "head", None),
    )
    return jax.shard_map(
        body,
        mesh=mesh,
        in_specs=placed,
        out_specs=(P(("groups", "dp", "pair"), "head", None), P(("groups", "dp", "pair"), "head")),
        check_vma=False,
    )
```

```python
import functools

import jax
import jax.numpy as jnp
from jax import lax
from jax.experimental import pallas as pl
from jax.experimental.pallas import tpu as pltpu
from jax.sharding import PartitionSpec as P

LANES = 128
BF16 = jnp.bfloat16
F32 = jnp.float32


def attend_kernel(capacity, heads, lengths_ref, queries_ref, keys_ref, values_ref, new_key_ref,
                  new_value_ref, routes_ref, weights_ref, out_ref, lhs_ref):
    row_count, head_count, head_size = queries_ref.shape
    kv_heads, cache_len = keys_ref.shape[1:3]
    grouping = head_count // kv_heads
    scaling = head_size ** (-0.5)
    contract = (((1,), (1,)), ((), ()))
    spans = [
        (r, g, slice(g * grouping, (g + 1) * grouping))
        for r in range(row_count)
        for g in range(kv_heads)
    ]
    scores, fresh, valid = [], [], []
    position = lax.broadcasted_iota(jnp.int32, (grouping, cache_len), 1)
    for r, g, part in spans:
        query = queries_ref[r, part]
        scores.append(
            lax.dot_general(query, keys_ref[r, g], contract, preferred_element_type=F32)
        )
        fresh.append(
            jnp.sum(
                query.astype(F32) * new_key_ref[r, g : g + 1].astype(F32), axis=1, keepdims=True
            )
        )
        valid.append(position < lengths_ref[r])
    fresh = jnp.concatenate(fresh, axis=0) * scaling
    scores = jnp.concatenate(
        [jnp.where(v, t * scaling, -1e30) for v, t in zip(valid, scores)], axis=0
    )
    highest = jnp.maximum(jnp.max(scores, axis=1, keepdims=True), fresh)
    weights = jnp.concatenate(
        [
            jnp.where(v, jnp.exp(scores[i * grouping : (i + 1) * grouping]
                                 - highest[i * grouping : (i + 1) * grouping]), 0.0)
            for i, v in enumerate(valid)
        ],
        axis=0,
    )
    fresh_weight = jnp.exp(fresh - highest)
    inverse = 1.0 / (jnp.sum(weights, axis=1, keepdims=True) + fresh_weight)
    rounded = weights.astype(BF16)
    fresh_rounded = fresh_weight.astype(BF16).astype(F32)
    for i, (r, g, part) in enumerate(spans):
        here = slice(i * grouping, (i + 1) * grouping)
        summed = jnp.dot(rounded[here], values_ref[r, g], preferred_element_type=F32)
        summed = summed + fresh_rounded[here] * new_value_ref[r, g : g + 1].astype(F32)
        out_ref[r, part] = (summed * inverse[here]).astype(BF16)

    dev_rows, route_count = routes_ref.shape
    total = lhs_ref.shape[1]
    lane = lax.broadcasted_iota(jnp.int32, (dev_rows, total), 1)
    expert = lane // (8 * heads)
    member = jnp.zeros((dev_rows, total), F32)
    rest = jnp.zeros((dev_rows, total), F32)
    for j in range(route_count):
        named = routes_ref[:, j : j + 1] == expert
        member = jnp.where(named, 1.0, member)
        rest = jnp.where(named, weights_ref[:, j : j + 1], rest)
    above = lax.broadcasted_iota(jnp.int32, (dev_rows, dev_rows), 0)
    below = lax.broadcasted_iota(jnp.int32, (dev_rows, dev_rows), 1)
    earlier = jnp.where(below < above, 1.0, 0.0).astype(BF16)
    rank = jnp.dot(earlier, member.astype(BF16), preferred_element_type=F32)
    taken = (member > 0.5) & (rank == (lane % capacity).astype(F32))
    rest = jnp.where(taken, rest, 0.0)
    cut = lane % 8 // capacity
    terms = []
    for _ in range(3):
        term = rest.astype(BF16).astype(F32)
        terms.append(term)
        rest = rest - term
    lhs_ref[...] = jnp.concatenate(
        [jnp.where(cut == k, term, 0.0) for k in range(8 // capacity) for term in terms], axis=0
    ).astype(BF16)


def attend(lengths, queries, key_cache, value_cache, new_key, new_value, routes, gate_weights,
           capacity, heads, sources):
    dev_rows = routes.shape[0]
    vmem = pl.BlockSpec(memory_space=pltpu.VMEM)
    return pl.pallas_call(
        functools.partial(attend_kernel, capacity, heads),
        out_shape=(
            jax.ShapeDtypeStruct(queries.shape, BF16),
            jax.ShapeDtypeStruct((8 // capacity * 3 * dev_rows, sources * heads * 8), BF16),
        ),
        in_specs=[pl.BlockSpec(memory_space=pltpu.SMEM)] + [vmem] * 7,
        out_specs=(vmem, vmem),
        compiler_params=pltpu.CompilerParams(vmem_limit_bytes=16 * 1024 * 1024),
        cost_estimate=pl.CostEstimate(flops=10**9, bytes_accessed=10**6, transcendentals=0),
    )(lengths, queries, key_cache, value_cache, new_key, new_value, routes, gate_weights)


def ffn_kernel(dims, order, place_ref, *refs):
    capacity, heads, route_count, dev_rows = dims
    row_refs, (gate, up, down, out_ref) = refs[:-4], refs[-4:]
    hidden_size, width = gate.shape[1:]
    share = width // heads
    pieces = 8 // capacity
    my_dp, my_pair = place_ref[0], place_ref[1]
    steps = len(order)
    sources = 2 * steps
    rows = sources * dev_rows

    names = jnp.concatenate([ref[:, width:] for ref in row_refs], axis=0)
    lane = lax.broadcasted_iota(jnp.int32, names.shape, 1)
    expert = (2 * my_dp + my_pair).astype(F32)
    named = jnp.where((lane < route_count) & (names.astype(F32) == expert), 1.0, 0.0).astype(BF16)
    member = lax.dot_general(
        jnp.ones((8, names.shape[1]), BF16), named, (((1,), (1,)), ((), ())),
        preferred_element_type=F32,
    )
    above = lax.broadcasted_iota(jnp.int32, (rows, rows), 0)
    below = lax.broadcasted_iota(jnp.int32, (rows, rows), 1)
    earlier = (above < below) & (above // dev_rows == below // dev_rows)
    rank = jnp.dot(
        member.astype(BF16), jnp.where(earlier, 1.0, 0.0).astype(BF16), preferred_element_type=F32
    )
    block = lax.broadcasted_iota(jnp.int32, member.shape, 1) // dev_rows
    step = jnp.zeros(member.shape, jnp.int32)
    for j in range(steps):
        step = jnp.where(block % steps == j, order[j], step)
    home = 2 * (my_dp ^ step) + jnp.where(block < steps, my_pair, 1 - my_pair)
    target = jnp.where(member > 0.5, home * capacity + rank.astype(jnp.int32), -1)
    spot = lax.broadcasted_iota(jnp.int32, (sources * 8, rows), 0)
    spot = spot // 8 * capacity + spot % capacity
    placing = jnp.where(spot == target[0:1], 1.0, 0.0).astype(BF16)

    inputs = jnp.concatenate([ref[:, :width] for ref in row_refs], axis=0)
    contract = (((1,), (1,)), ((), ()))
    chunk = 128 if hidden_size % 128 == 0 else hidden_size
    parts = []
    for start in range(0, hidden_size, chunk):
        part = slice(start, start + chunk)
        gate_part = lax.dot_general(inputs, gate[0, part], contract, preferred_element_type=F32)
        up_part = lax.dot_general(inputs, up[0, part], contract, preferred_element_type=F32)
        parts.append((gate_part / (1.0 + jnp.exp(-gate_part)) * up_part).astype(BF16))
    hidden = jnp.concatenate(parts, axis=1)
    hidden = jnp.dot(placing, hidden, preferred_element_type=F32).astype(BF16)

    piece = share // pieces
    cut = lax.broadcasted_iota(jnp.int32, (sources * 8, piece), 0) % 8 // capacity
    for h in range(heads):
        packed = None
        for k in range(pieces):
            start = h * share + k * piece
            result = jnp.dot(
                hidden, down[0, :, start : start + piece], preferred_element_type=F32
            )
            packed = result if packed is None else jnp.where(cut == k, result, packed)
        packed = packed.astype(BF16)
        for q in range(sources):
            out_ref[q * heads + h] = packed[q * 8 : q * 8 + 8]


def place_kernel(out_ref):
    out_ref[0] = lax.axis_index("dp")
    out_ref[1] = lax.axis_index("pair")


def my_place():
    return pl.pallas_call(
        place_kernel,
        out_shape=jax.ShapeDtypeStruct((2,), jnp.int32),
        out_specs=pl.BlockSpec(memory_space=pltpu.SMEM),
        compiler_params=pltpu.CompilerParams(vmem_limit_bytes=1024 * 1024),
        cost_estimate=pl.CostEstimate(flops=2 * 10**10, bytes_accessed=64, transcendentals=0),
    )()


def expert_block(place, rows, gate_matrix, up_matrix, down_matrix, order, capacity, heads,
                 route_count, dev_rows):
    sources = 2 * len(order)
    hidden_size, width = gate_matrix.shape[1:]
    piece = width // heads * capacity // 8
    vmem = pl.BlockSpec(memory_space=pltpu.VMEM)
    return pl.pallas_call(
        functools.partial(ffn_kernel, (capacity, heads, route_count, dev_rows), order),
        out_shape=jax.ShapeDtypeStruct((sources * heads, 8, piece), BF16),
        in_specs=[pl.BlockSpec(memory_space=pltpu.SMEM)] + [vmem] * (len(rows) + 3),
        out_specs=vmem,
        compiler_params=pltpu.CompilerParams(vmem_limit_bytes=32 * 1024 * 1024),
        cost_estimate=pl.CostEstimate(
            flops=2 * sources * 8 * width * hidden_size * 3,
            bytes_accessed=hidden_size * width * 6,
            transcendentals=sources * 8 * hidden_size,
        ),
    )(place, *rows, gate_matrix, up_matrix, down_matrix)


def combine_kernel(pieces, terms, lhs_ref, got_ref, out_ref):
    blocks, rows, piece = got_ref.shape
    got = got_ref[...].reshape(blocks * rows, piece)
    sums = jnp.dot(lhs_ref[...], got, preferred_element_type=F32)
    height = out_ref.shape[0]
    for k in range(pieces):
        total = None
        for t in range(terms):
            start = (k * terms + t) * height
            term = sums[start : start + height]
            total = term if total is None else total + term
        out_ref[:, k * piece : (k + 1) * piece] = total.astype(BF16)


def body(
    queries,
    key_cache,
    value_cache,
    new_key,
    new_value,
    lengths,
    expert_input,
    routes,
    gate_weights,
    gate_matrix,
    up_matrix,
    down_matrix,
):
    dev_rows, route_count = routes.shape
    width = expert_input.shape[1]
    steps, pairs, heads = lax.axis_size("dp"), lax.axis_size("pair"), lax.axis_size("head")
    sources = steps * pairs
    capacity = max(2, dev_rows * route_count // sources)
    pieces = 8 // capacity

    labels = jnp.pad(routes, ((0, 0), (0, LANES - route_count))).astype(BF16)
    block = jnp.concatenate([expert_input, labels], axis=1)

    def exchange(rows, step):
        return lax.ppermute(rows, "dp", [(i, i ^ step) for i in range(steps)])

    def other_core(rows):
        return lax.ppermute(rows, "pair", [(i, i ^ 1) for i in range(pairs)])

    even = sorted(range(2, steps, 2), reverse=True)
    direct = {step: exchange(block, step) for step in even + [1]}
    far, near = even[: len(even) * 2 // 3], even[len(even) * 2 // 3 :]
    near_rows = jnp.concatenate([direct[step] for step in near], axis=0)
    far_rows = jnp.concatenate([direct[step] for step in far], axis=0)
    near_on, far_on = exchange(near_rows, 1), exchange(far_rows, 1)
    mine = [block, direct[1], near_rows, near_on, far_rows, far_on]
    order = [0, 1] + near + [s ^ 1 for s in near] + far + [s ^ 1 for s in far]
    place = my_place()

    attention, lhs = attend(
        lengths, queries, key_cache, value_cache, new_key, new_value, routes, gate_weights,
        capacity, heads, sources,
    )
    sent = expert_block(
        place, mine + [other_core(rows) for rows in mine], gate_matrix, up_matrix,
        down_matrix, order, capacity, heads, route_count, dev_rows,
    )
    got = lax.all_to_all(sent, ("dp", "pair", "head"), split_axis=0, concat_axis=0, tiled=True)

    expert_output = pl.pallas_call(
        functools.partial(combine_kernel, pieces, 3),
        out_shape=jax.ShapeDtypeStruct((dev_rows, width // heads), BF16),
        compiler_params=pltpu.CompilerParams(vmem_limit_bytes=8 * 1024 * 1024),
    )(lhs, got)
    return (attention, expert_output)


def solution(mesh):
    placed = (
        P(("groups", "dp", "pair"), "head", None),
        P(("groups", "dp", "pair"), "head", None, None),
        P(("groups", "dp", "pair"), "head", None, None),
        P(("groups", "dp", "pair"), "head", None),
        P(("groups", "dp", "pair"), "head", None),
        P(("groups", "dp", "pair")),
        P(("groups", "dp", "pair"), None),
        P(("groups", "dp", "pair"), None),
        P(("groups", "dp", "pair"), None),
        P(("dp", "pair"), "head", None),
        P(("dp", "pair"), "head", None),
        P(("dp", "pair"), "head", None),
    )
    return jax.shard_map(
        body,
        mesh=mesh,
        in_specs=placed,
        out_specs=(P(("groups", "dp", "pair"), "head", None), P(("groups", "dp", "pair"), "head")),
        check_vma=False,
    )
```

```python
import functools

import jax
import jax.numpy as jnp
from jax import lax
from jax.experimental import pallas as pl
from jax.experimental.pallas import tpu as pltpu
from jax.sharding import PartitionSpec as P

LANES = 128
BF16 = jnp.bfloat16
F32 = jnp.float32


def attend_kernel(capacity, heads, lengths_ref, queries_ref, keys_ref, values_ref, new_key_ref,
                  new_value_ref, routes_ref, weights_ref, out_ref, lhs_ref):
    row_count, head_count, head_size = queries_ref.shape
    kv_heads, cache_len = keys_ref.shape[1:3]
    grouping = head_count // kv_heads
    scaling = head_size ** (-0.5)
    contract = (((1,), (1,)), ((), ()))
    spans = [
        (r, g, slice(g * grouping, (g + 1) * grouping))
        for r in range(row_count)
        for g in range(kv_heads)
    ]
    scores, fresh, valid = [], [], []
    position = lax.broadcasted_iota(jnp.int32, (grouping, cache_len), 1)
    for r, g, part in spans:
        query = queries_ref[r, part]
        scores.append(
            lax.dot_general(query, keys_ref[r, g], contract, preferred_element_type=F32)
        )
        fresh.append(
            jnp.sum(
                query.astype(F32) * new_key_ref[r, g : g + 1].astype(F32), axis=1, keepdims=True
            )
        )
        valid.append(position < lengths_ref[r])
    fresh = jnp.concatenate(fresh, axis=0) * scaling
    scores = jnp.concatenate(
        [jnp.where(v, t * scaling, -1e30) for v, t in zip(valid, scores)], axis=0
    )
    highest = jnp.maximum(jnp.max(scores, axis=1, keepdims=True), fresh)
    weights = jnp.concatenate(
        [
            jnp.where(v, jnp.exp(scores[i * grouping : (i + 1) * grouping]
                                 - highest[i * grouping : (i + 1) * grouping]), 0.0)
            for i, v in enumerate(valid)
        ],
        axis=0,
    )
    fresh_weight = jnp.exp(fresh - highest)
    inverse = 1.0 / (jnp.sum(weights, axis=1, keepdims=True) + fresh_weight)
    rounded = weights.astype(BF16)
    fresh_rounded = fresh_weight.astype(BF16).astype(F32)
    for i, (r, g, part) in enumerate(spans):
        here = slice(i * grouping, (i + 1) * grouping)
        summed = jnp.dot(rounded[here], values_ref[r, g], preferred_element_type=F32)
        summed = summed + fresh_rounded[here] * new_value_ref[r, g : g + 1].astype(F32)
        out_ref[r, part] = (summed * inverse[here]).astype(BF16)

    dev_rows, route_count = routes_ref.shape
    total = lhs_ref.shape[1]
    lane = lax.broadcasted_iota(jnp.int32, (dev_rows, total), 1)
    expert = lane // (8 * heads)
    member = jnp.zeros((dev_rows, total), F32)
    rest = jnp.zeros((dev_rows, total), F32)
    for j in range(route_count):
        named = routes_ref[:, j : j + 1] == expert
        member = jnp.where(named, 1.0, member)
        rest = jnp.where(named, weights_ref[:, j : j + 1], rest)
    above = lax.broadcasted_iota(jnp.int32, (dev_rows, dev_rows), 0)
    below = lax.broadcasted_iota(jnp.int32, (dev_rows, dev_rows), 1)
    earlier = jnp.where(below < above, 1.0, 0.0).astype(BF16)
    rank = jnp.dot(earlier, member.astype(BF16), preferred_element_type=F32)
    taken = (member > 0.5) & (rank == (lane % capacity).astype(F32))
    rest = jnp.where(taken, rest, 0.0)
    cut = lane % 8 // capacity
    terms = []
    for _ in range(3):
        term = rest.astype(BF16).astype(F32)
        terms.append(term)
        rest = rest - term
    lhs_ref[...] = jnp.concatenate(
        [jnp.where(cut == k, term, 0.0) for k in range(8 // capacity) for term in terms], axis=0
    ).astype(BF16)


def attend(lengths, queries, key_cache, value_cache, new_key, new_value, routes, gate_weights,
           capacity, heads, sources):
    dev_rows = routes.shape[0]
    vmem = pl.BlockSpec(memory_space=pltpu.VMEM)
    return pl.pallas_call(
        functools.partial(attend_kernel, capacity, heads),
        out_shape=(
            jax.ShapeDtypeStruct(queries.shape, BF16),
            jax.ShapeDtypeStruct((8 // capacity * 3 * dev_rows, sources * heads * 8), BF16),
        ),
        in_specs=[pl.BlockSpec(memory_space=pltpu.SMEM)] + [vmem] * 7,
        out_specs=(vmem, vmem),
        compiler_params=pltpu.CompilerParams(vmem_limit_bytes=16 * 1024 * 1024),
        cost_estimate=pl.CostEstimate(flops=10**9, bytes_accessed=10**6, transcendentals=0),
    )(lengths, queries, key_cache, value_cache, new_key, new_value, routes, gate_weights)


def ffn_kernel(dims, order, place_ref, *refs):
    capacity, heads, route_count, dev_rows = dims
    row_refs, (gate, up, down, out_ref) = refs[:-4], refs[-4:]
    hidden_size, width = gate.shape[1:]
    share = width // heads
    pieces = 8 // capacity
    my_dp, my_pair = place_ref[0], place_ref[1]
    steps = len(order)
    sources = 2 * steps
    rows = sources * dev_rows

    names = jnp.concatenate([ref[:, width:] for ref in row_refs], axis=0)
    lane = lax.broadcasted_iota(jnp.int32, names.shape, 1)
    expert = (2 * my_dp + my_pair).astype(F32)
    named = jnp.where((lane < route_count) & (names.astype(F32) == expert), 1.0, 0.0).astype(BF16)
    member = lax.dot_general(
        jnp.ones((8, names.shape[1]), BF16), named, (((1,), (1,)), ((), ())),
        preferred_element_type=F32,
    )
    above = lax.broadcasted_iota(jnp.int32, (rows, rows), 0)
    below = lax.broadcasted_iota(jnp.int32, (rows, rows), 1)
    earlier = (above < below) & (above // dev_rows == below // dev_rows)
    rank = jnp.dot(
        member.astype(BF16), jnp.where(earlier, 1.0, 0.0).astype(BF16), preferred_element_type=F32
    )
    block = lax.broadcasted_iota(jnp.int32, member.shape, 1) // dev_rows
    step = jnp.zeros(member.shape, jnp.int32)
    for j in range(steps):
        step = jnp.where(block % steps == j, order[j], step)
    home = 2 * (my_dp ^ step) + jnp.where(block < steps, my_pair, 1 - my_pair)
    target = jnp.where(member > 0.5, home * capacity + rank.astype(jnp.int32), -1)
    spot = lax.broadcasted_iota(jnp.int32, (sources * 8, rows), 0)
    spot = spot // 8 * capacity + spot % capacity
    placing = jnp.where(spot == target[0:1], 1.0, 0.0).astype(BF16)

    inputs = jnp.concatenate([ref[:, :width] for ref in row_refs], axis=0)
    contract = (((1,), (1,)), ((), ()))
    chunk = 128 if hidden_size % 128 == 0 else hidden_size
    parts = []
    for start in range(0, hidden_size, chunk):
        part = slice(start, start + chunk)
        gate_part = lax.dot_general(inputs, gate[0, part], contract, preferred_element_type=F32)
        up_part = lax.dot_general(inputs, up[0, part], contract, preferred_element_type=F32)
        parts.append((gate_part / (1.0 + jnp.exp(-gate_part)) * up_part).astype(BF16))
    hidden = jnp.concatenate(parts, axis=1)
    hidden = jnp.dot(placing, hidden, preferred_element_type=F32).astype(BF16)

    piece = share // pieces
    cut = lax.broadcasted_iota(jnp.int32, (sources * 8, piece), 0) % 8 // capacity
    for h in range(heads):
        packed = None
        for k in range(pieces):
            start = h * share + k * piece
            result = jnp.dot(
                hidden, down[0, :, start : start + piece], preferred_element_type=F32
            )
            packed = result if packed is None else jnp.where(cut == k, result, packed)
        packed = packed.astype(BF16)
        for q in range(sources):
            out_ref[q * heads + h] = packed[q * 8 : q * 8 + 8]


def place_kernel(out_ref):
    out_ref[0] = lax.axis_index("dp")
    out_ref[1] = lax.axis_index("pair")


def my_place():
    return pl.pallas_call(
        place_kernel,
        out_shape=jax.ShapeDtypeStruct((2,), jnp.int32),
        out_specs=pl.BlockSpec(memory_space=pltpu.SMEM),
        compiler_params=pltpu.CompilerParams(vmem_limit_bytes=1024 * 1024),
        cost_estimate=pl.CostEstimate(flops=2 * 10**10, bytes_accessed=64, transcendentals=0),
    )()


def expert_block(place, rows, gate_matrix, up_matrix, down_matrix, order, capacity, heads,
                 route_count, dev_rows):
    sources = 2 * len(order)
    hidden_size, width = gate_matrix.shape[1:]
    piece = width // heads * capacity // 8
    vmem = pl.BlockSpec(memory_space=pltpu.VMEM)
    return pl.pallas_call(
        functools.partial(ffn_kernel, (capacity, heads, route_count, dev_rows), order),
        out_shape=jax.ShapeDtypeStruct((sources * heads, 8, piece), BF16),
        in_specs=[pl.BlockSpec(memory_space=pltpu.SMEM)] + [vmem] * (len(rows) + 3),
        out_specs=vmem,
        compiler_params=pltpu.CompilerParams(vmem_limit_bytes=32 * 1024 * 1024),
        cost_estimate=pl.CostEstimate(
            flops=2 * sources * 8 * width * hidden_size * 3,
            bytes_accessed=hidden_size * width * 6,
            transcendentals=sources * 8 * hidden_size,
        ),
    )(place, *rows, gate_matrix, up_matrix, down_matrix)


def combine_kernel(pieces, terms, lhs_ref, got_ref, out_ref):
    blocks, rows, piece = got_ref.shape
    got = got_ref[...].reshape(blocks * rows, piece)
    sums = jnp.dot(lhs_ref[...], got, preferred_element_type=F32)
    height = out_ref.shape[0]
    for k in range(pieces):
        total = None
        for t in range(terms):
            start = (k * terms + t) * height
            term = sums[start : start + height]
            total = term if total is None else total + term
        out_ref[:, k * piece : (k + 1) * piece] = total.astype(BF16)


def body(
    queries,
    key_cache,
    value_cache,
    new_key,
    new_value,
    lengths,
    expert_input,
    routes,
    gate_weights,
    gate_matrix,
    up_matrix,
    down_matrix,
):
    dev_rows, route_count = routes.shape
    width = expert_input.shape[1]
    steps, pairs, heads = lax.axis_size("dp"), lax.axis_size("pair"), lax.axis_size("head")
    sources = steps * pairs
    capacity = max(2, dev_rows * route_count // sources)
    pieces = 8 // capacity

    labels = jnp.pad(routes, ((0, 0), (0, LANES - route_count))).astype(BF16)
    block = jnp.concatenate([expert_input, labels], axis=1)

    def exchange(rows, step):
        return lax.ppermute(rows, "dp", [(i, i ^ step) for i in range(steps)])

    def other_core(rows):
        return lax.ppermute(rows, "pair", [(i, i ^ 1) for i in range(pairs)])

    even = sorted(range(2, steps, 2), reverse=True)
    far = even[: len(even) * 2 // 3]
    near = [s + odd for s in even[len(far) :] for odd in (0, 1)] + [1]
    direct = {step: exchange(block, step) for step in far + near}
    place = my_place()
    near_rows = jnp.concatenate([block] + [direct[step] for step in near], axis=0)
    mine = [near_rows] + [direct[step] for step in far]
    mine = mine + [exchange(direct[step], 1) for step in far]
    order = [0] + near + far + [s ^ 1 for s in far]

    attention, lhs = attend(
        lengths, queries, key_cache, value_cache, new_key, new_value, routes, gate_weights,
        capacity, heads, sources,
    )
    sent = expert_block(
        place, mine + [other_core(rows) for rows in mine],
        gate_matrix, up_matrix,
        down_matrix, order, capacity, heads, route_count, dev_rows,
    )
    got = lax.all_to_all(sent, ("dp", "pair", "head"), split_axis=0, concat_axis=0, tiled=True)

    expert_output = pl.pallas_call(
        functools.partial(combine_kernel, pieces, 3),
        out_shape=jax.ShapeDtypeStruct((dev_rows, width // heads), BF16),
        compiler_params=pltpu.CompilerParams(vmem_limit_bytes=8 * 1024 * 1024),
    )(lhs, got)
    return (attention, expert_output)


def solution(mesh):
    placed = (
        P(("groups", "dp", "pair"), "head", None),
        P(("groups", "dp", "pair"), "head", None, None),
        P(("groups", "dp", "pair"), "head", None, None),
        P(("groups", "dp", "pair"), "head", None),
        P(("groups", "dp", "pair"), "head", None),
        P(("groups", "dp", "pair")),
        P(("groups", "dp", "pair"), None),
        P(("groups", "dp", "pair"), None),
        P(("groups", "dp", "pair"), None),
        P(("dp", "pair"), "head", None),
        P(("dp", "pair"), "head", None),
        P(("dp", "pair"), "head", None),
    )
    return jax.shard_map(
        body,
        mesh=mesh,
        in_specs=placed,
        out_specs=(P(("groups", "dp", "pair"), "head", None), P(("groups", "dp", "pair"), "head")),
        check_vma=False,
    )
```

```python
import functools

import jax
import jax.numpy as jnp
from jax import lax
from jax.experimental import pallas as pl
from jax.experimental.pallas import tpu as pltpu
from jax.sharding import PartitionSpec as P

LANES = 128
BF16 = jnp.bfloat16
F32 = jnp.float32


def attend_kernel(capacity, heads, lengths_ref, queries_ref, keys_ref, values_ref, new_key_ref,
                  new_value_ref, routes_ref, weights_ref, out_ref, lhs_ref):
    row_count, head_count, head_size = queries_ref.shape
    kv_heads, cache_len = keys_ref.shape[1:3]
    grouping = head_count // kv_heads
    scaling = head_size ** (-0.5)
    contract = (((1,), (1,)), ((), ()))
    spans = [
        (r, g, slice(g * grouping, (g + 1) * grouping))
        for r in range(row_count)
        for g in range(kv_heads)
    ]
    scores, fresh, valid = [], [], []
    position = lax.broadcasted_iota(jnp.int32, (grouping, cache_len), 1)
    for r, g, part in spans:
        query = queries_ref[r, part]
        scores.append(
            lax.dot_general(query, keys_ref[r, g], contract, preferred_element_type=F32)
        )
        fresh.append(
            jnp.sum(
                query.astype(F32) * new_key_ref[r, g : g + 1].astype(F32), axis=1, keepdims=True
            )
        )
        valid.append(position < lengths_ref[r])
    fresh = jnp.concatenate(fresh, axis=0) * scaling
    scores = jnp.concatenate(
        [jnp.where(v, t * scaling, -1e30) for v, t in zip(valid, scores)], axis=0
    )
    highest = jnp.maximum(jnp.max(scores, axis=1, keepdims=True), fresh)
    weights = jnp.concatenate(
        [
            jnp.where(v, jnp.exp(scores[i * grouping : (i + 1) * grouping]
                                 - highest[i * grouping : (i + 1) * grouping]), 0.0)
            for i, v in enumerate(valid)
        ],
        axis=0,
    )
    fresh_weight = jnp.exp(fresh - highest)
    inverse = 1.0 / (jnp.sum(weights, axis=1, keepdims=True) + fresh_weight)
    rounded = weights.astype(BF16)
    fresh_rounded = fresh_weight.astype(BF16).astype(F32)
    for i, (r, g, part) in enumerate(spans):
        here = slice(i * grouping, (i + 1) * grouping)
        summed = jnp.dot(rounded[here], values_ref[r, g], preferred_element_type=F32)
        summed = summed + fresh_rounded[here] * new_value_ref[r, g : g + 1].astype(F32)
        out_ref[r, part] = (summed * inverse[here]).astype(BF16)

    dev_rows, route_count = routes_ref.shape
    total = lhs_ref.shape[1]
    lane = lax.broadcasted_iota(jnp.int32, (dev_rows, total), 1)
    expert = lane // (8 * heads)
    member = jnp.zeros((dev_rows, total), F32)
    rest = jnp.zeros((dev_rows, total), F32)
    for j in range(route_count):
        named = routes_ref[:, j : j + 1] == expert
        member = jnp.where(named, 1.0, member)
        rest = jnp.where(named, weights_ref[:, j : j + 1], rest)
    above = lax.broadcasted_iota(jnp.int32, (dev_rows, dev_rows), 0)
    below = lax.broadcasted_iota(jnp.int32, (dev_rows, dev_rows), 1)
    earlier = jnp.where(below < above, 1.0, 0.0).astype(BF16)
    rank = jnp.dot(earlier, member.astype(BF16), preferred_element_type=F32)
    taken = (member > 0.5) & (rank == (lane % capacity).astype(F32))
    rest = jnp.where(taken, rest, 0.0)
    cut = lane % 8 // capacity
    terms = []
    for _ in range(3):
        term = rest.astype(BF16).astype(F32)
        terms.append(term)
        rest = rest - term
    lhs_ref[...] = jnp.concatenate(
        [jnp.where(cut == k, term, 0.0) for k in range(8 // capacity) for term in terms], axis=0
    ).astype(BF16)


def attend(lengths, queries, key_cache, value_cache, new_key, new_value, routes, gate_weights,
           capacity, heads, sources):
    dev_rows = routes.shape[0]
    vmem = pl.BlockSpec(memory_space=pltpu.VMEM)
    return pl.pallas_call(
        functools.partial(attend_kernel, capacity, heads),
        out_shape=(
            jax.ShapeDtypeStruct(queries.shape, BF16),
            jax.ShapeDtypeStruct((8 // capacity * 3 * dev_rows, sources * heads * 8), BF16),
        ),
        in_specs=[pl.BlockSpec(memory_space=pltpu.SMEM)] + [vmem] * 7,
        out_specs=(vmem, vmem),
        compiler_params=pltpu.CompilerParams(vmem_limit_bytes=16 * 1024 * 1024),
        cost_estimate=pl.CostEstimate(flops=10**9, bytes_accessed=10**6, transcendentals=0),
    )(lengths, queries, key_cache, value_cache, new_key, new_value, routes, gate_weights)


def ffn_kernel(dims, order, dp_ref, pair_ref, *refs):
    capacity, heads, route_count, dev_rows = dims
    row_refs, (gate, up, down, out_ref) = refs[:-4], refs[-4:]
    hidden_size, width = gate.shape[1:]
    share = width // heads
    pieces = 8 // capacity
    my_dp, my_pair = dp_ref[0:1, 0:1], pair_ref[0:1, 0:1]
    steps = len(order)
    sources = 2 * steps
    rows = sources * dev_rows

    inputs = jnp.concatenate([ref[:, :width] for ref in row_refs], axis=0)
    contract = (((1,), (1,)), ((), ()))
    chunk = 128 if hidden_size % 128 == 0 else hidden_size
    parts = []
    for start in range(0, hidden_size, chunk):
        part = slice(start, start + chunk)
        gate_part = lax.dot_general(inputs, gate[0, part], contract, preferred_element_type=F32)
        up_part = lax.dot_general(inputs, up[0, part], contract, preferred_element_type=F32)
        parts.append((gate_part / (1.0 + jnp.exp(-gate_part)) * up_part).astype(BF16))
    hidden = jnp.concatenate(parts, axis=1)
    names = jnp.concatenate([ref[:, width:] for ref in row_refs], axis=0)
    lane = lax.broadcasted_iota(jnp.int32, names.shape, 1)
    expert = (2 * my_dp + my_pair).astype(F32)
    named = jnp.where((lane < route_count) & (names.astype(F32) == expert), 1.0, 0.0).astype(BF16)
    member = lax.dot_general(
        jnp.ones((8, names.shape[1]), BF16), named, (((1,), (1,)), ((), ())),
        preferred_element_type=F32,
    )
    above = lax.broadcasted_iota(jnp.int32, (rows, rows), 0)
    below = lax.broadcasted_iota(jnp.int32, (rows, rows), 1)
    earlier = (above < below) & (above // dev_rows == below // dev_rows)
    rank = jnp.dot(
        member.astype(BF16), jnp.where(earlier, 1.0, 0.0).astype(BF16), preferred_element_type=F32
    )
    block = lax.broadcasted_iota(jnp.int32, member.shape, 1) // dev_rows
    step = jnp.zeros(member.shape, jnp.int32)
    for j in range(steps):
        step = jnp.where(block % steps == j, order[j], step)
    home = 2 * (my_dp ^ step) + jnp.where(block < steps, my_pair, 1 - my_pair)
    target = jnp.where(member > 0.5, home * capacity + rank.astype(jnp.int32), -1)
    spot = lax.broadcasted_iota(jnp.int32, (sources * 8, rows), 0)
    spot = spot // 8 * capacity + spot % capacity
    placing = jnp.where(spot == target[0:1], 1.0, 0.0).astype(BF16)
    hidden = jnp.dot(placing, hidden, preferred_element_type=F32).astype(BF16)

    piece = share // pieces
    cut = lax.broadcasted_iota(jnp.int32, (sources * 8, piece), 0) % 8 // capacity
    for h in range(heads):
        packed = None
        for k in range(pieces):
            start = h * share + k * piece
            result = jnp.dot(
                hidden, down[0, :, start : start + piece], preferred_element_type=F32
            )
            packed = result if packed is None else jnp.where(cut == k, result, packed)
        packed = packed.astype(BF16)
        for q in range(sources):
            out_ref[q * heads + h] = packed[q * 8 : q * 8 + 8]


def place_kernel(axis, out_ref):
    out_ref[...] = jnp.full(out_ref.shape, lax.axis_index(axis), jnp.int32)


def my_place(axis, flops):
    return pl.pallas_call(
        functools.partial(place_kernel, axis),
        out_shape=jax.ShapeDtypeStruct((8, LANES), jnp.int32),
        compiler_params=pltpu.CompilerParams(vmem_limit_bytes=1024 * 1024),
        cost_estimate=pl.CostEstimate(flops=flops, bytes_accessed=64, transcendentals=0),
    )()


def expert_block(place, rows, gate_matrix, up_matrix, down_matrix, order, capacity, heads,
                 route_count, dev_rows):
    sources = 2 * len(order)
    hidden_size, width = gate_matrix.shape[1:]
    piece = width // heads * capacity // 8
    vmem = pl.BlockSpec(memory_space=pltpu.VMEM)
    return pl.pallas_call(
        functools.partial(ffn_kernel, (capacity, heads, route_count, dev_rows), order),
        out_shape=jax.ShapeDtypeStruct((sources * heads, 8, piece), BF16),
        in_specs=[vmem] * (len(rows) + 5),
        out_specs=vmem,
        compiler_params=pltpu.CompilerParams(vmem_limit_bytes=32 * 1024 * 1024),
        cost_estimate=pl.CostEstimate(
            flops=2 * sources * 8 * width * hidden_size * 3,
            bytes_accessed=hidden_size * width * 6,
            transcendentals=sources * 8 * hidden_size,
        ),
    )(*place, *rows, gate_matrix, up_matrix, down_matrix)


def combine_kernel(pieces, terms, lhs_ref, got_ref, out_ref):
    blocks, rows, piece = got_ref.shape
    got = got_ref[...].reshape(blocks * rows, piece)
    sums = jnp.dot(lhs_ref[...], got, preferred_element_type=F32)
    height = out_ref.shape[0]
    for k in range(pieces):
        total = None
        for t in range(terms):
            start = (k * terms + t) * height
            term = sums[start : start + height]
            total = term if total is None else total + term
        out_ref[:, k * piece : (k + 1) * piece] = total.astype(BF16)


def body(
    queries,
    key_cache,
    value_cache,
    new_key,
    new_value,
    lengths,
    expert_input,
    routes,
    gate_weights,
    gate_matrix,
    up_matrix,
    down_matrix,
):
    dev_rows, route_count = routes.shape
    width = expert_input.shape[1]
    steps, pairs, heads = lax.axis_size("dp"), lax.axis_size("pair"), lax.axis_size("head")
    sources = steps * pairs
    capacity = max(2, dev_rows * route_count // sources)
    pieces = 8 // capacity

    my_pair, routes = lax.optimization_barrier((my_place("pair", 10**10), routes))
    labels = jnp.pad(routes, ((0, 0), (0, LANES - route_count))).astype(BF16)
    block = jnp.concatenate([expert_input, labels], axis=1)

    def exchange(rows, step):
        return lax.ppermute(rows, "dp", [(i, i ^ step) for i in range(steps)])

    def other_core(rows):
        return lax.ppermute(rows, "pair", [(i, i ^ 1) for i in range(pairs)])

    even = sorted(range(2, steps, 2), reverse=True)
    far = even[: len(even) * 2 // 3]
    near = [s + odd for s in even[len(far) :] for odd in (0, 1)] + [1]
    direct = {step: exchange(block, step) for step in far + near}
    place = (my_place("dp", 2 * 10**10), my_pair)
    near_rows = jnp.concatenate([block] + [direct[step] for step in near], axis=0)
    mine = [near_rows] + [direct[step] for step in far]
    mine = mine + [exchange(direct[step], 1) for step in far]
    order = [0] + near + far + [s ^ 1 for s in far]

    attention, lhs = attend(
        lengths, queries, key_cache, value_cache, new_key, new_value, routes, gate_weights,
        capacity, heads, sources,
    )
    sent = expert_block(
        place, mine + [other_core(rows) for rows in mine],
        gate_matrix, up_matrix,
        down_matrix, order, capacity, heads, route_count, dev_rows,
    )
    got = lax.all_to_all(sent, ("dp", "pair", "head"), split_axis=0, concat_axis=0, tiled=True)

    expert_output = pl.pallas_call(
        functools.partial(combine_kernel, pieces, 3),
        out_shape=jax.ShapeDtypeStruct((dev_rows, width // heads), BF16),
        compiler_params=pltpu.CompilerParams(vmem_limit_bytes=8 * 1024 * 1024),
    )(lhs, got)
    return (attention, expert_output)


def solution(mesh):
    placed = (
        P(("groups", "dp", "pair"), "head", None),
        P(("groups", "dp", "pair"), "head", None, None),
        P(("groups", "dp", "pair"), "head", None, None),
        P(("groups", "dp", "pair"), "head", None),
        P(("groups", "dp", "pair"), "head", None),
        P(("groups", "dp", "pair")),
        P(("groups", "dp", "pair"), None),
        P(("groups", "dp", "pair"), None),
        P(("groups", "dp", "pair"), None),
        P(("dp", "pair"), "head", None),
        P(("dp", "pair"), "head", None),
        P(("dp", "pair"), "head", None),
    )
    return jax.shard_map(
        body,
        mesh=mesh,
        in_specs=placed,
        out_specs=(P(("groups", "dp", "pair"), "head", None), P(("groups", "dp", "pair"), "head")),
        check_vma=False,
    )
```

```python
import functools

import jax
import jax.numpy as jnp
from jax import lax
from jax.experimental import pallas as pl
from jax.experimental.pallas import tpu as pltpu
from jax.sharding import PartitionSpec as P

LANES = 128
BF16 = jnp.bfloat16
F32 = jnp.float32


def attend_kernel(capacity, heads, lengths_ref, queries_ref, keys_ref, values_ref, new_key_ref,
                  new_value_ref, routes_ref, weights_ref, out_ref, lhs_ref):
    row_count, head_count, head_size = queries_ref.shape
    kv_heads, cache_len = keys_ref.shape[1:3]
    grouping = head_count // kv_heads
    scaling = head_size ** (-0.5)
    contract = (((1,), (1,)), ((), ()))
    spans = [
        (r, g, slice(g * grouping, (g + 1) * grouping))
        for r in range(row_count)
        for g in range(kv_heads)
    ]
    scores, fresh, valid = [], [], []
    position = lax.broadcasted_iota(jnp.int32, (grouping, cache_len), 1)
    for r, g, part in spans:
        query = queries_ref[r, part]
        scores.append(
            lax.dot_general(query, keys_ref[r, g], contract, preferred_element_type=F32)
        )
        fresh.append(
            jnp.sum(
                query.astype(F32) * new_key_ref[r, g : g + 1].astype(F32), axis=1, keepdims=True
            )
        )
        valid.append(position < lengths_ref[r])
    fresh = jnp.concatenate(fresh, axis=0) * scaling
    scores = jnp.concatenate(
        [jnp.where(v, t * scaling, -1e30) for v, t in zip(valid, scores)], axis=0
    )
    highest = jnp.maximum(jnp.max(scores, axis=1, keepdims=True), fresh)
    weights = jnp.concatenate(
        [
            jnp.where(v, jnp.exp(scores[i * grouping : (i + 1) * grouping]
                                 - highest[i * grouping : (i + 1) * grouping]), 0.0)
            for i, v in enumerate(valid)
        ],
        axis=0,
    )
    fresh_weight = jnp.exp(fresh - highest)
    inverse = 1.0 / (jnp.sum(weights, axis=1, keepdims=True) + fresh_weight)
    rounded = weights.astype(BF16)
    fresh_rounded = fresh_weight.astype(BF16).astype(F32)
    for i, (r, g, part) in enumerate(spans):
        here = slice(i * grouping, (i + 1) * grouping)
        summed = jnp.dot(rounded[here], values_ref[r, g], preferred_element_type=F32)
        summed = summed + fresh_rounded[here] * new_value_ref[r, g : g + 1].astype(F32)
        out_ref[r, part] = (summed * inverse[here]).astype(BF16)

    dev_rows, route_count = routes_ref.shape
    total = lhs_ref.shape[1]
    lane = lax.broadcasted_iota(jnp.int32, (dev_rows, total), 1)
    expert = lane // (8 * heads)
    member = jnp.zeros((dev_rows, total), F32)
    rest = jnp.zeros((dev_rows, total), F32)
    for j in range(route_count):
        named = routes_ref[:, j : j + 1] == expert
        member = jnp.where(named, 1.0, member)
        rest = jnp.where(named, weights_ref[:, j : j + 1], rest)
    above = lax.broadcasted_iota(jnp.int32, (dev_rows, dev_rows), 0)
    below = lax.broadcasted_iota(jnp.int32, (dev_rows, dev_rows), 1)
    earlier = jnp.where(below < above, 1.0, 0.0).astype(BF16)
    rank = jnp.dot(earlier, member.astype(BF16), preferred_element_type=F32)
    taken = (member > 0.5) & (rank == (lane % capacity).astype(F32))
    rest = jnp.where(taken, rest, 0.0)
    cut = lane % 8 // capacity
    terms = []
    for _ in range(3):
        term = rest.astype(BF16).astype(F32)
        terms.append(term)
        rest = rest - term
    lhs_ref[...] = jnp.concatenate(
        [jnp.where(cut == k, term, 0.0) for k in range(8 // capacity) for term in terms], axis=0
    ).astype(BF16)


def attend(lengths, queries, key_cache, value_cache, new_key, new_value, routes, gate_weights,
           capacity, heads, sources):
    dev_rows = routes.shape[0]
    vmem = pl.BlockSpec(memory_space=pltpu.VMEM)
    return pl.pallas_call(
        functools.partial(attend_kernel, capacity, heads),
        out_shape=(
            jax.ShapeDtypeStruct(queries.shape, BF16),
            jax.ShapeDtypeStruct((8 // capacity * 3 * dev_rows, sources * heads * 8), BF16),
        ),
        in_specs=[pl.BlockSpec(memory_space=pltpu.SMEM)] + [vmem] * 7,
        out_specs=(vmem, vmem),
        compiler_params=pltpu.CompilerParams(vmem_limit_bytes=16 * 1024 * 1024),
        cost_estimate=pl.CostEstimate(flops=10**9, bytes_accessed=10**6, transcendentals=0),
    )(lengths, queries, key_cache, value_cache, new_key, new_value, routes, gate_weights)


def ffn_kernel(dims, order, dp_ref, pair_ref, *refs):
    capacity, heads, route_count, dev_rows = dims
    row_refs, (gate, up, down, out_ref) = refs[:-4], refs[-4:]
    hidden_size, width = gate.shape[1:]
    share = width // heads
    pieces = 8 // capacity
    my_dp, my_pair = dp_ref[0:1, 0:1], pair_ref[0:1, 0:1]
    steps = len(order)
    sources = 2 * steps
    rows = sources * dev_rows

    inputs = jnp.concatenate([ref[:, :width] for ref in row_refs], axis=0)
    contract = (((1,), (1,)), ((), ()))
    chunk = 128 if hidden_size % 128 == 0 else hidden_size
    parts = []
    for start in range(0, hidden_size, chunk):
        part = slice(start, start + chunk)
        gate_part = lax.dot_general(inputs, gate[0, part], contract, preferred_element_type=F32)
        up_part = lax.dot_general(inputs, up[0, part], contract, preferred_element_type=F32)
        parts.append((gate_part / (1.0 + jnp.exp(-gate_part)) * up_part).astype(BF16))
    hidden = jnp.concatenate(parts, axis=1)
    names = jnp.concatenate([ref[:, width:] for ref in row_refs], axis=0)
    lane = lax.broadcasted_iota(jnp.int32, names.shape, 1)
    expert = (2 * my_dp + my_pair).astype(F32)
    named = jnp.where((lane < route_count) & (names.astype(F32) == expert), 1.0, 0.0).astype(BF16)
    member = lax.dot_general(
        jnp.ones((8, names.shape[1]), BF16), named, (((1,), (1,)), ((), ())),
        preferred_element_type=F32,
    )
    above = lax.broadcasted_iota(jnp.int32, (rows, rows), 0)
    below = lax.broadcasted_iota(jnp.int32, (rows, rows), 1)
    earlier = (above < below) & (above // dev_rows == below // dev_rows)
    rank = jnp.dot(
        member.astype(BF16), jnp.where(earlier, 1.0, 0.0).astype(BF16), preferred_element_type=F32
    )
    block = lax.broadcasted_iota(jnp.int32, member.shape, 1) // dev_rows
    step = jnp.zeros(member.shape, jnp.int32)
    for j in range(steps):
        step = jnp.where(block % steps == j, order[j], step)
    home = 2 * (my_dp ^ step) + jnp.where(block < steps, my_pair, 1 - my_pair)
    target = jnp.where(member > 0.5, home * capacity + rank.astype(jnp.int32), -1)
    spot = lax.broadcasted_iota(jnp.int32, (sources * 8, rows), 0)
    spot = spot // 8 * capacity + spot % capacity
    placing = jnp.where(spot == target[0:1], 1.0, 0.0).astype(BF16)
    hidden = jnp.dot(placing, hidden, preferred_element_type=F32).astype(BF16)

    piece = share // pieces
    cut = lax.broadcasted_iota(jnp.int32, (sources * 8, piece), 0) % 8 // capacity
    for h in range(heads):
        packed = None
        for k in range(pieces):
            start = h * share + k * piece
            result = jnp.dot(
                hidden, down[0, :, start : start + piece], preferred_element_type=F32
            )
            packed = result if packed is None else jnp.where(cut == k, result, packed)
        packed = packed.astype(BF16)
        for q in range(sources):
            out_ref[q * heads + h] = packed[q * 8 : q * 8 + 8]


def place_kernel(axis, out_ref):
    out_ref[...] = jnp.full(out_ref.shape, lax.axis_index(axis), jnp.int32)


def my_place(axis, flops):
    return pl.pallas_call(
        functools.partial(place_kernel, axis),
        out_shape=jax.ShapeDtypeStruct((8, LANES), jnp.int32),
        compiler_params=pltpu.CompilerParams(vmem_limit_bytes=1024 * 1024),
        cost_estimate=pl.CostEstimate(flops=flops, bytes_accessed=64, transcendentals=0),
    )()


def expert_block(place, rows, gate_matrix, up_matrix, down_matrix, order, capacity, heads,
                 route_count, dev_rows):
    sources = 2 * len(order)
    hidden_size, width = gate_matrix.shape[1:]
    piece = width // heads * capacity // 8
    vmem = pl.BlockSpec(memory_space=pltpu.VMEM)
    return pl.pallas_call(
        functools.partial(ffn_kernel, (capacity, heads, route_count, dev_rows), order),
        out_shape=jax.ShapeDtypeStruct((sources * heads, 8, piece), BF16),
        in_specs=[vmem] * (len(rows) + 5),
        out_specs=vmem,
        compiler_params=pltpu.CompilerParams(vmem_limit_bytes=32 * 1024 * 1024),
        cost_estimate=pl.CostEstimate(
            flops=2 * sources * 8 * width * hidden_size * 3,
            bytes_accessed=hidden_size * width * 6,
            transcendentals=sources * 8 * hidden_size,
        ),
    )(*place, *rows, gate_matrix, up_matrix, down_matrix)


def combine_kernel(pieces, terms, lhs_ref, got_ref, out_ref):
    blocks, rows, piece = got_ref.shape
    got = got_ref[...].reshape(blocks * rows, piece)
    sums = jnp.dot(lhs_ref[...], got, preferred_element_type=F32)
    height = out_ref.shape[0]
    for k in range(pieces):
        total = None
        for t in range(terms):
            start = (k * terms + t) * height
            term = sums[start : start + height]
            total = term if total is None else total + term
        out_ref[:, k * piece : (k + 1) * piece] = total.astype(BF16)


def body(
    queries,
    key_cache,
    value_cache,
    new_key,
    new_value,
    lengths,
    expert_input,
    routes,
    gate_weights,
    gate_matrix,
    up_matrix,
    down_matrix,
):
    dev_rows, route_count = routes.shape
    width = expert_input.shape[1]
    steps, pairs, heads = lax.axis_size("dp"), lax.axis_size("pair"), lax.axis_size("head")
    sources = steps * pairs
    capacity = max(2, dev_rows * route_count // sources)
    pieces = 8 // capacity

    my_pair, routes = lax.optimization_barrier((my_place("pair", 10**10), routes))
    labels = jnp.pad(routes, ((0, 0), (0, LANES - route_count))).astype(BF16)
    block = jnp.concatenate([expert_input, labels], axis=1)

    def exchange(rows, step):
        return lax.ppermute(rows, "dp", [(i, i ^ step) for i in range(steps)])

    def other_core(rows):
        return lax.ppermute(rows, "pair", [(i, i ^ 1) for i in range(pairs)])

    even = sorted(range(2, steps, 2), reverse=True)
    far = even[: len(even) * 2 // 3]
    near = [s + odd for s in even[len(far) :] for odd in (0, 1)] + [1]
    direct = {step: exchange(block, step) for step in far + near}
    place = (my_place("dp", 2 * 10**10), my_pair)
    near_rows = jnp.concatenate([block] + [direct[step] for step in near], axis=0)
    mine = [near_rows] + [direct[step] for step in far]
    mine = mine + [exchange(direct[far[0]], 1)] + [exchange(block, step ^ 1) for step in far[1:]]
    order = [0] + near + far + [s ^ 1 for s in far]

    attention, lhs = attend(
        lengths, queries, key_cache, value_cache, new_key, new_value, routes, gate_weights,
        capacity, heads, sources,
    )
    sent = expert_block(
        place, mine + [other_core(rows) for rows in mine],
        gate_matrix, up_matrix,
        down_matrix, order, capacity, heads, route_count, dev_rows,
    )
    got = lax.all_to_all(sent, ("dp", "pair", "head"), split_axis=0, concat_axis=0, tiled=True)

    expert_output = pl.pallas_call(
        functools.partial(combine_kernel, pieces, 3),
        out_shape=jax.ShapeDtypeStruct((dev_rows, width // heads), BF16),
        compiler_params=pltpu.CompilerParams(vmem_limit_bytes=8 * 1024 * 1024),
    )(lhs, got)
    return (attention, expert_output)


def solution(mesh):
    placed = (
        P(("groups", "dp", "pair"), "head", None),
        P(("groups", "dp", "pair"), "head", None, None),
        P(("groups", "dp", "pair"), "head", None, None),
        P(("groups", "dp", "pair"), "head", None),
        P(("groups", "dp", "pair"), "head", None),
        P(("groups", "dp", "pair")),
        P(("groups", "dp", "pair"), None),
        P(("groups", "dp", "pair"), None),
        P(("groups", "dp", "pair"), None),
        P(("dp", "pair"), "head", None),
        P(("dp", "pair"), "head", None),
        P(("dp", "pair"), "head", None),
    )
    return jax.shard_map(
        body,
        mesh=mesh,
        in_specs=placed,
        out_specs=(P(("groups", "dp", "pair"), "head", None), P(("groups", "dp", "pair"), "head")),
        check_vma=False,
    )
```

```python
import functools

import jax
import jax.numpy as jnp
from jax import lax
from jax.experimental import pallas as pl
from jax.experimental.pallas import tpu as pltpu
from jax.sharding import PartitionSpec as P

LANES = 128
BF16 = jnp.bfloat16
F32 = jnp.float32


def attend_kernel(capacity, heads, lengths_ref, queries_ref, keys_ref, values_ref, new_key_ref,
                  new_value_ref, routes_ref, weights_ref, out_ref, lhs_ref):
    row_count, head_count, head_size = queries_ref.shape
    kv_heads, cache_len = keys_ref.shape[1:3]
    grouping = head_count // kv_heads
    scaling = head_size ** (-0.5)
    contract = (((1,), (1,)), ((), ()))
    spans = [
        (r, g, slice(g * grouping, (g + 1) * grouping))
        for r in range(row_count)
        for g in range(kv_heads)
    ]
    scores, fresh, valid = [], [], []
    position = lax.broadcasted_iota(jnp.int32, (grouping, cache_len), 1)
    for r, g, part in spans:
        query = queries_ref[r, part]
        scores.append(
            lax.dot_general(query, keys_ref[r, g], contract, preferred_element_type=F32)
        )
        fresh.append(
            jnp.sum(
                query.astype(F32) * new_key_ref[r, g : g + 1].astype(F32), axis=1, keepdims=True
            )
        )
        valid.append(position < lengths_ref[r])
    fresh = jnp.concatenate(fresh, axis=0) * scaling
    scores = jnp.concatenate(
        [jnp.where(v, t * scaling, -1e30) for v, t in zip(valid, scores)], axis=0
    )
    highest = jnp.maximum(jnp.max(scores, axis=1, keepdims=True), fresh)
    weights = jnp.concatenate(
        [
            jnp.where(v, jnp.exp(scores[i * grouping : (i + 1) * grouping]
                                 - highest[i * grouping : (i + 1) * grouping]), 0.0)
            for i, v in enumerate(valid)
        ],
        axis=0,
    )
    fresh_weight = jnp.exp(fresh - highest)
    inverse = 1.0 / (jnp.sum(weights, axis=1, keepdims=True) + fresh_weight)
    rounded = weights.astype(BF16)
    fresh_rounded = fresh_weight.astype(BF16).astype(F32)
    for i, (r, g, part) in enumerate(spans):
        here = slice(i * grouping, (i + 1) * grouping)
        summed = jnp.dot(rounded[here], values_ref[r, g], preferred_element_type=F32)
        summed = summed + fresh_rounded[here] * new_value_ref[r, g : g + 1].astype(F32)
        out_ref[r, part] = (summed * inverse[here]).astype(BF16)

    dev_rows, route_count = routes_ref.shape
    total = lhs_ref.shape[1]
    lane = lax.broadcasted_iota(jnp.int32, (dev_rows, total), 1)
    expert = lane // (8 * heads)
    member = jnp.zeros((dev_rows, total), F32)
    rest = jnp.zeros((dev_rows, total), F32)
    for j in range(route_count):
        named = routes_ref[:, j : j + 1] == expert
        member = jnp.where(named, 1.0, member)
        rest = jnp.where(named, weights_ref[:, j : j + 1], rest)
    above = lax.broadcasted_iota(jnp.int32, (dev_rows, dev_rows), 0)
    below = lax.broadcasted_iota(jnp.int32, (dev_rows, dev_rows), 1)
    earlier = jnp.where(below < above, 1.0, 0.0).astype(BF16)
    rank = jnp.dot(earlier, member.astype(BF16), preferred_element_type=F32)
    taken = (member > 0.5) & (rank == (lane % capacity).astype(F32))
    rest = jnp.where(taken, rest, 0.0)
    cut = lane % 8 // capacity
    terms = []
    for _ in range(3):
        term = rest.astype(BF16).astype(F32)
        terms.append(term)
        rest = rest - term
    lhs_ref[...] = jnp.concatenate(
        [jnp.where(cut == k, term, 0.0) for k in range(8 // capacity) for term in terms], axis=0
    ).astype(BF16)


def attend(lengths, queries, key_cache, value_cache, new_key, new_value, routes, gate_weights,
           capacity, heads, sources):
    dev_rows = routes.shape[0]
    vmem = pl.BlockSpec(memory_space=pltpu.VMEM)
    return pl.pallas_call(
        functools.partial(attend_kernel, capacity, heads),
        out_shape=(
            jax.ShapeDtypeStruct(queries.shape, BF16),
            jax.ShapeDtypeStruct((8 // capacity * 3 * dev_rows, sources * heads * 8), BF16),
        ),
        in_specs=[pl.BlockSpec(memory_space=pltpu.SMEM)] + [vmem] * 7,
        out_specs=(vmem, vmem),
        compiler_params=pltpu.CompilerParams(vmem_limit_bytes=16 * 1024 * 1024),
        cost_estimate=pl.CostEstimate(flops=10**9, bytes_accessed=10**6, transcendentals=0),
    )(lengths, queries, key_cache, value_cache, new_key, new_value, routes, gate_weights)


def ffn_kernel(dims, order, dp_ref, pair_ref, *refs):
    capacity, heads, route_count, dev_rows = dims
    row_refs, (gate, up, down, out_ref) = refs[:-4], refs[-4:]
    hidden_size, width = gate.shape[1:]
    share = width // heads
    pieces = 8 // capacity
    my_dp, my_pair = dp_ref[0:1, 0:1], pair_ref[0:1, 0:1]
    steps = len(order)
    sources = 2 * steps
    rows = sources * dev_rows

    inputs = jnp.concatenate([ref[:, :width] for ref in row_refs], axis=0)
    contract = (((1,), (1,)), ((), ()))
    chunk = 128 if hidden_size % 128 == 0 else hidden_size
    parts = []
    for start in range(0, hidden_size, chunk):
        part = slice(start, start + chunk)
        gate_part = lax.dot_general(inputs, gate[0, part], contract, preferred_element_type=F32)
        up_part = lax.dot_general(inputs, up[0, part], contract, preferred_element_type=F32)
        parts.append((gate_part / (1.0 + jnp.exp(-gate_part)) * up_part).astype(BF16))
    hidden = jnp.concatenate(parts, axis=1)
    names = jnp.concatenate([ref[:, width:] for ref in row_refs], axis=0)
    lane = lax.broadcasted_iota(jnp.int32, names.shape, 1)
    expert = (2 * my_dp + my_pair).astype(F32)
    named = jnp.where((lane < route_count) & (names.astype(F32) == expert), 1.0, 0.0).astype(BF16)
    member = lax.dot_general(
        jnp.ones((8, names.shape[1]), BF16), named, (((1,), (1,)), ((), ())),
        preferred_element_type=F32,
    )
    above = lax.broadcasted_iota(jnp.int32, (rows, rows), 0)
    below = lax.broadcasted_iota(jnp.int32, (rows, rows), 1)
    earlier = (above < below) & (above // dev_rows == below // dev_rows)
    rank = jnp.dot(
        member.astype(BF16), jnp.where(earlier, 1.0, 0.0).astype(BF16), preferred_element_type=F32
    )
    block = lax.broadcasted_iota(jnp.int32, member.shape, 1) // dev_rows
    step = jnp.zeros(member.shape, jnp.int32)
    for j in range(steps):
        step = jnp.where(block % steps == j, order[j], step)
    home = 2 * (my_dp ^ step) + jnp.where(block < steps, my_pair, 1 - my_pair)
    target = jnp.where(member > 0.5, home * capacity + rank.astype(jnp.int32), -1)
    spot = lax.broadcasted_iota(jnp.int32, (sources * 8, rows), 0)
    spot = spot // 8 * capacity + spot % capacity
    placing = jnp.where(spot == target[0:1], 1.0, 0.0).astype(BF16)
    hidden = jnp.dot(placing, hidden, preferred_element_type=F32).astype(BF16)

    piece = share // pieces
    cut = lax.broadcasted_iota(jnp.int32, (sources * 8, piece), 0) % 8 // capacity
    for h in range(heads):
        packed = None
        for k in range(pieces):
            start = h * share + k * piece
            result = jnp.dot(
                hidden, down[0, :, start : start + piece], preferred_element_type=F32
            )
            packed = result if packed is None else jnp.where(cut == k, result, packed)
        packed = packed.astype(BF16)
        for q in range(sources):
            out_ref[q * heads + h] = packed[q * 8 : q * 8 + 8]


def place_kernel(axis, out_ref):
    out_ref[...] = jnp.full(out_ref.shape, lax.axis_index(axis), jnp.int32)


def my_place(axis, flops):
    return pl.pallas_call(
        functools.partial(place_kernel, axis),
        out_shape=jax.ShapeDtypeStruct((8, LANES), jnp.int32),
        compiler_params=pltpu.CompilerParams(vmem_limit_bytes=1024 * 1024),
        cost_estimate=pl.CostEstimate(flops=flops, bytes_accessed=64, transcendentals=0),
    )()


def expert_block(place, rows, gate_matrix, up_matrix, down_matrix, order, capacity, heads,
                 route_count, dev_rows):
    sources = 2 * len(order)
    hidden_size, width = gate_matrix.shape[1:]
    piece = width // heads * capacity // 8
    vmem = pl.BlockSpec(memory_space=pltpu.VMEM)
    return pl.pallas_call(
        functools.partial(ffn_kernel, (capacity, heads, route_count, dev_rows), order),
        out_shape=jax.ShapeDtypeStruct((sources * heads, 8, piece), BF16),
        in_specs=[vmem] * (len(rows) + 5),
        out_specs=vmem,
        compiler_params=pltpu.CompilerParams(vmem_limit_bytes=32 * 1024 * 1024),
        cost_estimate=pl.CostEstimate(
            flops=2 * sources * 8 * width * hidden_size * 3,
            bytes_accessed=hidden_size * width * 6,
            transcendentals=sources * 8 * hidden_size,
        ),
    )(*place, *rows, gate_matrix, up_matrix, down_matrix)


def combine_kernel(pieces, terms, lhs_ref, got_ref, out_ref):
    blocks, rows, piece = got_ref.shape
    got = got_ref[...].reshape(blocks * rows, piece)
    sums = jnp.dot(lhs_ref[...], got, preferred_element_type=F32)
    height = out_ref.shape[0]
    for k in range(pieces):
        total = None
        for t in range(terms):
            start = (k * terms + t) * height
            term = sums[start : start + height]
            total = term if total is None else total + term
        out_ref[:, k * piece : (k + 1) * piece] = total.astype(BF16)


def body(
    queries,
    key_cache,
    value_cache,
    new_key,
    new_value,
    lengths,
    expert_input,
    routes,
    gate_weights,
    gate_matrix,
    up_matrix,
    down_matrix,
):
    dev_rows, route_count = routes.shape
    width = expert_input.shape[1]
    steps, pairs, heads = lax.axis_size("dp"), lax.axis_size("pair"), lax.axis_size("head")
    sources = steps * pairs
    capacity = max(2, dev_rows * route_count // sources)
    pieces = 8 // capacity

    my_pair, routes = lax.optimization_barrier((my_place("pair", 10**10), routes))
    labels = jnp.pad(routes, ((0, 0), (0, LANES - route_count))).astype(BF16)
    block = jnp.concatenate([expert_input, labels], axis=1)

    def exchange(rows, step):
        return lax.ppermute(rows, "dp", [(i, i ^ step) for i in range(steps)])

    def other_core(rows):
        return lax.ppermute(rows, "pair", [(i, i ^ 1) for i in range(pairs)])

    even = sorted(range(2, steps, 2), reverse=True)
    place = (my_place("dp", 2 * 10**10), my_pair)
    farthest = exchange(block, even[0])
    both = jnp.concatenate([block, exchange(block, 1)], axis=0)
    last = [s ^ odd for s in even[-1:] for odd in (0, 1)]
    mine = [both, farthest] + [exchange(block, step) for step in last]
    mine = mine + [exchange(both, step) for step in even[1:-1]] + [exchange(farthest, 1)]
    order = [0, 1, even[0]] + last + [s ^ odd for s in even[1:-1] for odd in (0, 1)] + [even[0] ^ 1]

    attention, lhs = attend(
        lengths, queries, key_cache, value_cache, new_key, new_value, routes, gate_weights,
        capacity, heads, sources,
    )
    sent = expert_block(
        place, mine + [other_core(rows) for rows in mine],
        gate_matrix, up_matrix,
        down_matrix, order, capacity, heads, route_count, dev_rows,
    )
    got = lax.all_to_all(sent, ("dp", "pair", "head"), split_axis=0, concat_axis=0, tiled=True)

    expert_output = pl.pallas_call(
        functools.partial(combine_kernel, pieces, 3),
        out_shape=jax.ShapeDtypeStruct((dev_rows, width // heads), BF16),
        compiler_params=pltpu.CompilerParams(vmem_limit_bytes=8 * 1024 * 1024),
    )(lhs, got)
    return (attention, expert_output)


def solution(mesh):
    placed = (
        P(("groups", "dp", "pair"), "head", None),
        P(("groups", "dp", "pair"), "head", None, None),
        P(("groups", "dp", "pair"), "head", None, None),
        P(("groups", "dp", "pair"), "head", None),
        P(("groups", "dp", "pair"), "head", None),
        P(("groups", "dp", "pair")),
        P(("groups", "dp", "pair"), None),
        P(("groups", "dp", "pair"), None),
        P(("groups", "dp", "pair"), None),
        P(("dp", "pair"), "head", None),
        P(("dp", "pair"), "head", None),
        P(("dp", "pair"), "head", None),
    )
    return jax.shard_map(
        body,
        mesh=mesh,
        in_specs=placed,
        out_specs=(P(("groups", "dp", "pair"), "head", None), P(("groups", "dp", "pair"), "head")),
        check_vma=False,
    )
```

```python
import functools

import jax
import jax.numpy as jnp
from jax import lax
from jax.experimental import pallas as pl
from jax.experimental.pallas import tpu as pltpu
from jax.sharding import PartitionSpec as P

LANES = 128
BF16 = jnp.bfloat16
F32 = jnp.float32


def attend_kernel(capacity, heads, lengths_ref, queries_ref, keys_ref, values_ref, new_key_ref,
                  new_value_ref, routes_ref, weights_ref, out_ref, lhs_ref):
    row_count, head_count, head_size = queries_ref.shape
    kv_heads, cache_len = keys_ref.shape[1:3]
    grouping = head_count // kv_heads
    scaling = head_size ** (-0.5)
    contract = (((1,), (1,)), ((), ()))
    spans = [
        (r, g, slice(g * grouping, (g + 1) * grouping))
        for r in range(row_count)
        for g in range(kv_heads)
    ]
    scores, fresh, valid = [], [], []
    position = lax.broadcasted_iota(jnp.int32, (grouping, cache_len), 1)
    for r, g, part in spans:
        query = queries_ref[r, part]
        scores.append(
            lax.dot_general(query, keys_ref[r, g], contract, preferred_element_type=F32)
        )
        fresh.append(
            jnp.sum(
                query.astype(F32) * new_key_ref[r, g : g + 1].astype(F32), axis=1, keepdims=True
            )
        )
        valid.append(position < lengths_ref[r])
    fresh = jnp.concatenate(fresh, axis=0) * scaling
    scores = jnp.concatenate(
        [jnp.where(v, t * scaling, -1e30) for v, t in zip(valid, scores)], axis=0
    )
    highest = jnp.maximum(jnp.max(scores, axis=1, keepdims=True), fresh)
    weights = jnp.concatenate(
        [
            jnp.where(v, jnp.exp(scores[i * grouping : (i + 1) * grouping]
                                 - highest[i * grouping : (i + 1) * grouping]), 0.0)
            for i, v in enumerate(valid)
        ],
        axis=0,
    )
    fresh_weight = jnp.exp(fresh - highest)
    inverse = 1.0 / (jnp.sum(weights, axis=1, keepdims=True) + fresh_weight)
    rounded = weights.astype(BF16)
    fresh_rounded = fresh_weight.astype(BF16).astype(F32)
    for i, (r, g, part) in enumerate(spans):
        here = slice(i * grouping, (i + 1) * grouping)
        summed = jnp.dot(rounded[here], values_ref[r, g], preferred_element_type=F32)
        summed = summed + fresh_rounded[here] * new_value_ref[r, g : g + 1].astype(F32)
        out_ref[r, part] = (summed * inverse[here]).astype(BF16)

    dev_rows, route_count = routes_ref.shape
    total = lhs_ref.shape[1]
    lane = lax.broadcasted_iota(jnp.int32, (dev_rows, total), 1)
    expert = lane // (8 * heads)
    member = jnp.zeros((dev_rows, total), F32)
    rest = jnp.zeros((dev_rows, total), F32)
    for j in range(route_count):
        named = routes_ref[:, j : j + 1] == expert
        member = jnp.where(named, 1.0, member)
        rest = jnp.where(named, weights_ref[:, j : j + 1], rest)
    above = lax.broadcasted_iota(jnp.int32, (dev_rows, dev_rows), 0)
    below = lax.broadcasted_iota(jnp.int32, (dev_rows, dev_rows), 1)
    earlier = jnp.where(below < above, 1.0, 0.0).astype(BF16)
    rank = jnp.dot(earlier, member.astype(BF16), preferred_element_type=F32)
    taken = (member > 0.5) & (rank == (lane % capacity).astype(F32))
    rest = jnp.where(taken, rest, 0.0)
    cut = lane % 8 // capacity
    terms = []
    for _ in range(3):
        term = rest.astype(BF16).astype(F32)
        terms.append(term)
        rest = rest - term
    lhs_ref[...] = jnp.concatenate(
        [jnp.where(cut == k, term, 0.0) for k in range(8 // capacity) for term in terms], axis=0
    ).astype(BF16)


def attend(lengths, queries, key_cache, value_cache, new_key, new_value, routes, gate_weights,
           capacity, heads, sources):
    dev_rows = routes.shape[0]
    vmem = pl.BlockSpec(memory_space=pltpu.VMEM)
    return pl.pallas_call(
        functools.partial(attend_kernel, capacity, heads),
        out_shape=(
            jax.ShapeDtypeStruct(queries.shape, BF16),
            jax.ShapeDtypeStruct((8 // capacity * 3 * dev_rows, sources * heads * 8), BF16),
        ),
        in_specs=[pl.BlockSpec(memory_space=pltpu.SMEM)] + [vmem] * 7,
        out_specs=(vmem, vmem),
        compiler_params=pltpu.CompilerParams(vmem_limit_bytes=16 * 1024 * 1024),
        cost_estimate=pl.CostEstimate(flops=10**9, bytes_accessed=10**6, transcendentals=0),
    )(lengths, queries, key_cache, value_cache, new_key, new_value, routes, gate_weights)


def ffn_kernel(dims, order, dp_ref, pair_ref, *refs):
    capacity, heads, route_count, dev_rows = dims
    row_refs, (gate, up, down, out_ref) = refs[:-4], refs[-4:]
    hidden_size, width = gate.shape[1:]
    share = width // heads
    pieces = 8 // capacity
    my_dp, my_pair = dp_ref[0:1, 0:1], pair_ref[0:1, 0:1]
    steps = len(order)
    sources = 2 * steps
    rows = sources * dev_rows

    inputs = jnp.concatenate([ref[:, :width] for ref in row_refs], axis=0)
    contract = (((1,), (1,)), ((), ()))
    chunk = 128 if hidden_size % 128 == 0 else hidden_size
    parts = []
    for start in range(0, hidden_size, chunk):
        part = slice(start, start + chunk)
        gate_part = lax.dot_general(inputs, gate[0, part], contract, preferred_element_type=F32)
        up_part = lax.dot_general(inputs, up[0, part], contract, preferred_element_type=F32)
        parts.append((gate_part / (1.0 + jnp.exp(-gate_part)) * up_part).astype(BF16))
    hidden = jnp.concatenate(parts, axis=1)
    names = jnp.concatenate([ref[:, width:] for ref in row_refs], axis=0)
    lane = lax.broadcasted_iota(jnp.int32, names.shape, 1)
    expert = (2 * my_dp + my_pair).astype(F32)
    named = jnp.where((lane < route_count) & (names.astype(F32) == expert), 1.0, 0.0).astype(BF16)
    member = lax.dot_general(
        jnp.ones((8, names.shape[1]), BF16), named, (((1,), (1,)), ((), ())),
        preferred_element_type=F32,
    )
    above = lax.broadcasted_iota(jnp.int32, (rows, rows), 0)
    below = lax.broadcasted_iota(jnp.int32, (rows, rows), 1)
    earlier = (above < below) & (above // dev_rows == below // dev_rows)
    rank = jnp.dot(
        member.astype(BF16), jnp.where(earlier, 1.0, 0.0).astype(BF16), preferred_element_type=F32
    )
    block = lax.broadcasted_iota(jnp.int32, member.shape, 1) // dev_rows
    step = jnp.zeros(member.shape, jnp.int32)
    for j in range(steps):
        step = jnp.where(block % steps == j, order[j], step)
    home = 2 * (my_dp ^ step) + jnp.where(block < steps, my_pair, 1 - my_pair)
    target = jnp.where(member > 0.5, home * capacity + rank.astype(jnp.int32), -1)
    spot = lax.broadcasted_iota(jnp.int32, (sources * 8, rows), 0)
    spot = spot // 8 * capacity + spot % capacity
    placing = jnp.where(spot == target[0:1], 1.0, 0.0).astype(BF16)
    hidden = jnp.dot(placing, hidden, preferred_element_type=F32).astype(BF16)

    piece = share // pieces
    cut = lax.broadcasted_iota(jnp.int32, (sources * 8, piece), 0) % 8 // capacity
    for h in range(heads):
        packed = None
        for k in range(pieces):
            start = h * share + k * piece
            result = jnp.dot(
                hidden, down[0, :, start : start + piece], preferred_element_type=F32
            )
            packed = result if packed is None else jnp.where(cut == k, result, packed)
        packed = packed.astype(BF16)
        for q in range(sources):
            out_ref[q * heads + h] = packed[q * 8 : q * 8 + 8]


def place_kernel(axis, out_ref):
    out_ref[...] = jnp.full(out_ref.shape, lax.axis_index(axis), jnp.int32)


def my_place(axis, flops):
    return pl.pallas_call(
        functools.partial(place_kernel, axis),
        out_shape=jax.ShapeDtypeStruct((8, LANES), jnp.int32),
        compiler_params=pltpu.CompilerParams(vmem_limit_bytes=1024 * 1024),
        cost_estimate=pl.CostEstimate(flops=flops, bytes_accessed=64, transcendentals=0),
    )()


def expert_block(place, rows, gate_matrix, up_matrix, down_matrix, order, capacity, heads,
                 route_count, dev_rows):
    sources = 2 * len(order)
    hidden_size, width = gate_matrix.shape[1:]
    piece = width // heads * capacity // 8
    vmem = pl.BlockSpec(memory_space=pltpu.VMEM)
    return pl.pallas_call(
        functools.partial(ffn_kernel, (capacity, heads, route_count, dev_rows), order),
        out_shape=jax.ShapeDtypeStruct((sources * heads, 8, piece), BF16),
        in_specs=[vmem] * (len(rows) + 5),
        out_specs=vmem,
        compiler_params=pltpu.CompilerParams(vmem_limit_bytes=32 * 1024 * 1024),
        cost_estimate=pl.CostEstimate(
            flops=2 * sources * 8 * width * hidden_size * 3,
            bytes_accessed=hidden_size * width * 6,
            transcendentals=sources * 8 * hidden_size,
        ),
    )(*place, *rows, gate_matrix, up_matrix, down_matrix)


def combine_kernel(pieces, terms, lhs_ref, got_ref, out_ref):
    blocks, rows, piece = got_ref.shape
    got = got_ref[...].reshape(blocks * rows, piece)
    sums = jnp.dot(lhs_ref[...], got, preferred_element_type=F32)
    height = out_ref.shape[0]
    for k in range(pieces):
        total = None
        for t in range(terms):
            start = (k * terms + t) * height
            term = sums[start : start + height]
            total = term if total is None else total + term
        out_ref[:, k * piece : (k + 1) * piece] = total.astype(BF16)


def body(
    queries,
    key_cache,
    value_cache,
    new_key,
    new_value,
    lengths,
    expert_input,
    routes,
    gate_weights,
    gate_matrix,
    up_matrix,
    down_matrix,
):
    dev_rows, route_count = routes.shape
    width = expert_input.shape[1]
    steps, pairs, heads = lax.axis_size("dp"), lax.axis_size("pair"), lax.axis_size("head")
    sources = steps * pairs
    capacity = max(2, dev_rows * route_count // sources)
    pieces = 8 // capacity

    my_pair, routes = lax.optimization_barrier((my_place("pair", 10**10), routes))
    labels = jnp.pad(routes, ((0, 0), (0, LANES - route_count))).astype(BF16)
    block = jnp.concatenate([expert_input, labels], axis=1)

    def exchange(rows, step):
        return lax.ppermute(rows, "dp", [(i, i ^ step) for i in range(steps)])

    def other_core(rows):
        return lax.ppermute(rows, "pair", [(i, i ^ 1) for i in range(pairs)])

    even = sorted(range(2, steps, 2), reverse=True)
    place = (my_place("dp", 2 * 10**10), my_pair)
    farthest = exchange(block, even[0])
    both = jnp.concatenate([block, exchange(block, 1)], axis=0)
    mine = [both, farthest] + [exchange(both, step) for step in even[1:]] + [exchange(farthest, 1)]
    order = [0, 1, even[0]] + [s ^ odd for s in even[1:] for odd in (0, 1)] + [even[0] ^ 1]

    attention, lhs = attend(
        lengths, queries, key_cache, value_cache, new_key, new_value, routes, gate_weights,
        capacity, heads, sources,
    )
    sent = expert_block(
        place, mine + [other_core(rows) for rows in mine],
        gate_matrix, up_matrix,
        down_matrix, order, capacity, heads, route_count, dev_rows,
    )
    got = lax.all_to_all(sent, ("dp", "pair", "head"), split_axis=0, concat_axis=0, tiled=True)

    expert_output = pl.pallas_call(
        functools.partial(combine_kernel, pieces, 3),
        out_shape=jax.ShapeDtypeStruct((dev_rows, width // heads), BF16),
        compiler_params=pltpu.CompilerParams(vmem_limit_bytes=8 * 1024 * 1024),
    )(lhs, got)
    return (attention, expert_output)


def solution(mesh):
    placed = (
        P(("groups", "dp", "pair"), "head", None),
        P(("groups", "dp", "pair"), "head", None, None),
        P(("groups", "dp", "pair"), "head", None, None),
        P(("groups", "dp", "pair"), "head", None),
        P(("groups", "dp", "pair"), "head", None),
        P(("groups", "dp", "pair")),
        P(("groups", "dp", "pair"), None),
        P(("groups", "dp", "pair"), None),
        P(("groups", "dp", "pair"), None),
        P(("dp", "pair"), "head", None),
        P(("dp", "pair"), "head", None),
        P(("dp", "pair"), "head", None),
    )
    return jax.shard_map(
        body,
        mesh=mesh,
        in_specs=placed,
        out_specs=(P(("groups", "dp", "pair"), "head", None), P(("groups", "dp", "pair"), "head")),
        check_vma=False,
    )
```

```python
import functools

import jax
import jax.numpy as jnp
from jax import lax
from jax.experimental import pallas as pl
from jax.experimental.pallas import tpu as pltpu
from jax.sharding import PartitionSpec as P

LANES = 128
BF16 = jnp.bfloat16
F32 = jnp.float32


def attend_kernel(capacity, heads, lengths_ref, queries_ref, keys_ref, values_ref, new_key_ref,
                  new_value_ref, routes_ref, weights_ref, out_ref, lhs_ref):
    row_count, head_count, head_size = queries_ref.shape
    kv_heads, cache_len = keys_ref.shape[1:3]
    grouping = head_count // kv_heads
    scaling = head_size ** (-0.5)
    contract = (((1,), (1,)), ((), ()))
    spans = [
        (r, g, slice(g * grouping, (g + 1) * grouping))
        for r in range(row_count)
        for g in range(kv_heads)
    ]
    scores, fresh, valid = [], [], []
    position = lax.broadcasted_iota(jnp.int32, (grouping, cache_len), 1)
    for r, g, part in spans:
        query = queries_ref[r, part]
        scores.append(
            lax.dot_general(query, keys_ref[r, g], contract, preferred_element_type=F32)
        )
        fresh.append(
            jnp.sum(
                query.astype(F32) * new_key_ref[r, g : g + 1].astype(F32), axis=1, keepdims=True
            )
        )
        valid.append(position < lengths_ref[r])
    fresh = jnp.concatenate(fresh, axis=0) * scaling
    scores = jnp.concatenate(
        [jnp.where(v, t * scaling, -1e30) for v, t in zip(valid, scores)], axis=0
    )
    highest = jnp.maximum(jnp.max(scores, axis=1, keepdims=True), fresh)
    weights = jnp.concatenate(
        [
            jnp.where(v, jnp.exp(scores[i * grouping : (i + 1) * grouping]
                                 - highest[i * grouping : (i + 1) * grouping]), 0.0)
            for i, v in enumerate(valid)
        ],
        axis=0,
    )
    fresh_weight = jnp.exp(fresh - highest)
    inverse = 1.0 / (jnp.sum(weights, axis=1, keepdims=True) + fresh_weight)
    rounded = weights.astype(BF16)
    fresh_rounded = fresh_weight.astype(BF16).astype(F32)
    for i, (r, g, part) in enumerate(spans):
        here = slice(i * grouping, (i + 1) * grouping)
        summed = jnp.dot(rounded[here], values_ref[r, g], preferred_element_type=F32)
        summed = summed + fresh_rounded[here] * new_value_ref[r, g : g + 1].astype(F32)
        out_ref[r, part] = (summed * inverse[here]).astype(BF16)

    dev_rows, route_count = routes_ref.shape
    total = lhs_ref.shape[1]
    lane = lax.broadcasted_iota(jnp.int32, (dev_rows, total), 1)
    expert = lane // (8 * heads)
    member = jnp.zeros((dev_rows, total), F32)
    rest = jnp.zeros((dev_rows, total), F32)
    for j in range(route_count):
        named = routes_ref[:, j : j + 1] == expert
        member = jnp.where(named, 1.0, member)
        rest = jnp.where(named, weights_ref[:, j : j + 1], rest)
    above = lax.broadcasted_iota(jnp.int32, (dev_rows, dev_rows), 0)
    below = lax.broadcasted_iota(jnp.int32, (dev_rows, dev_rows), 1)
    earlier = jnp.where(below < above, 1.0, 0.0).astype(BF16)
    rank = jnp.dot(earlier, member.astype(BF16), preferred_element_type=F32)
    taken = (member > 0.5) & (rank == (lane % capacity).astype(F32))
    rest = jnp.where(taken, rest, 0.0)
    cut = lane % 8 // capacity
    terms = []
    for _ in range(3):
        term = rest.astype(BF16).astype(F32)
        terms.append(term)
        rest = rest - term
    lhs_ref[...] = jnp.concatenate(
        [jnp.where(cut == k, term, 0.0) for k in range(8 // capacity) for term in terms], axis=0
    ).astype(BF16)


def attend(lengths, queries, key_cache, value_cache, new_key, new_value, routes, gate_weights,
           capacity, heads, sources):
    dev_rows = routes.shape[0]
    vmem = pl.BlockSpec(memory_space=pltpu.VMEM)
    return pl.pallas_call(
        functools.partial(attend_kernel, capacity, heads),
        out_shape=(
            jax.ShapeDtypeStruct(queries.shape, BF16),
            jax.ShapeDtypeStruct((8 // capacity * 3 * dev_rows, sources * heads * 8), BF16),
        ),
        in_specs=[pl.BlockSpec(memory_space=pltpu.SMEM)] + [vmem] * 7,
        out_specs=(vmem, vmem),
        compiler_params=pltpu.CompilerParams(vmem_limit_bytes=16 * 1024 * 1024),
        cost_estimate=pl.CostEstimate(flops=10**9, bytes_accessed=10**6, transcendentals=0),
    )(lengths, queries, key_cache, value_cache, new_key, new_value, routes, gate_weights)


def ffn_kernel(dims, order, dp_ref, pair_ref, *refs):
    capacity, heads, route_count, dev_rows = dims
    row_refs, (gate, up, down, out_ref) = refs[:-4], refs[-4:]
    hidden_size, width = gate.shape[1:]
    share = width // heads
    pieces = 8 // capacity
    my_dp, my_pair = dp_ref[0:1, 0:1], pair_ref[0:1, 0:1]
    steps = len(order)
    sources = 2 * steps
    rows = sources * dev_rows

    inputs = jnp.concatenate([ref[:, :width] for ref in row_refs], axis=0)
    contract = (((1,), (1,)), ((), ()))
    chunk = 128 if hidden_size % 128 == 0 else hidden_size
    parts = []
    for start in range(0, hidden_size, chunk):
        part = slice(start, start + chunk)
        gate_part = lax.dot_general(inputs, gate[0, part], contract, preferred_element_type=F32)
        up_part = lax.dot_general(inputs, up[0, part], contract, preferred_element_type=F32)
        parts.append((gate_part / (1.0 + jnp.exp(-gate_part)) * up_part).astype(BF16))
    hidden = jnp.concatenate(parts, axis=1)
    names = jnp.concatenate([ref[:, width:] for ref in row_refs], axis=0)
    lane = lax.broadcasted_iota(jnp.int32, names.shape, 1)
    expert = (2 * my_dp + my_pair).astype(F32)
    named = jnp.where((lane < route_count) & (names.astype(F32) == expert), 1.0, 0.0).astype(BF16)
    member = lax.dot_general(
        jnp.ones((8, names.shape[1]), BF16), named, (((1,), (1,)), ((), ())),
        preferred_element_type=F32,
    )
    above = lax.broadcasted_iota(jnp.int32, (rows, rows), 0)
    below = lax.broadcasted_iota(jnp.int32, (rows, rows), 1)
    earlier = (above < below) & (above // dev_rows == below // dev_rows)
    rank = jnp.dot(
        member.astype(BF16), jnp.where(earlier, 1.0, 0.0).astype(BF16), preferred_element_type=F32
    )
    block = lax.broadcasted_iota(jnp.int32, member.shape, 1) // dev_rows
    step = jnp.zeros(member.shape, jnp.int32)
    for j in range(steps):
        step = jnp.where(block % steps == j, order[j], step)
    home = 2 * (my_dp ^ step) + jnp.where(block < steps, my_pair, 1 - my_pair)
    target = jnp.where(member > 0.5, home * capacity + rank.astype(jnp.int32), -1)
    spot = lax.broadcasted_iota(jnp.int32, (sources * 8, rows), 0)
    spot = spot // 8 * capacity + spot % capacity
    placing = jnp.where(spot == target[0:1], 1.0, 0.0).astype(BF16)
    hidden = jnp.dot(placing, hidden, preferred_element_type=F32).astype(BF16)

    piece = share // pieces
    cut = lax.broadcasted_iota(jnp.int32, (sources * 8, piece), 0) % 8 // capacity
    for h in range(heads):
        packed = None
        for k in range(pieces):
            start = h * share + k * piece
            result = jnp.dot(
                hidden, down[0, :, start : start + piece], preferred_element_type=F32
            )
            packed = result if packed is None else jnp.where(cut == k, result, packed)
        packed = packed.astype(BF16)
        for q in range(sources):
            out_ref[q * heads + h] = packed[q * 8 : q * 8 + 8]


def place_kernel(axis, out_ref):
    out_ref[...] = jnp.full(out_ref.shape, lax.axis_index(axis), jnp.int32)


def my_place(axis, flops):
    return pl.pallas_call(
        functools.partial(place_kernel, axis),
        out_shape=jax.ShapeDtypeStruct((8, LANES), jnp.int32),
        compiler_params=pltpu.CompilerParams(vmem_limit_bytes=1024 * 1024),
        cost_estimate=pl.CostEstimate(flops=flops, bytes_accessed=64, transcendentals=0),
    )()


def expert_block(place, rows, gate_matrix, up_matrix, down_matrix, order, capacity, heads,
                 route_count, dev_rows):
    sources = 2 * len(order)
    hidden_size, width = gate_matrix.shape[1:]
    piece = width // heads * capacity // 8
    vmem = pl.BlockSpec(memory_space=pltpu.VMEM)
    return pl.pallas_call(
        functools.partial(ffn_kernel, (capacity, heads, route_count, dev_rows), order),
        out_shape=jax.ShapeDtypeStruct((sources * heads, 8, piece), BF16),
        in_specs=[vmem] * (len(rows) + 5),
        out_specs=vmem,
        compiler_params=pltpu.CompilerParams(vmem_limit_bytes=32 * 1024 * 1024),
        cost_estimate=pl.CostEstimate(
            flops=2 * sources * 8 * width * hidden_size * 3,
            bytes_accessed=hidden_size * width * 6,
            transcendentals=sources * 8 * hidden_size,
        ),
    )(*place, *rows, gate_matrix, up_matrix, down_matrix)


def combine_kernel(pieces, terms, lhs_ref, got_ref, out_ref):
    blocks, rows, piece = got_ref.shape
    got = got_ref[...].reshape(blocks * rows, piece)
    sums = jnp.dot(lhs_ref[...], got, preferred_element_type=F32)
    height = out_ref.shape[0]
    for k in range(pieces):
        total = None
        for t in range(terms):
            start = (k * terms + t) * height
            term = sums[start : start + height]
            total = term if total is None else total + term
        out_ref[:, k * piece : (k + 1) * piece] = total.astype(BF16)


def body(
    queries,
    key_cache,
    value_cache,
    new_key,
    new_value,
    lengths,
    expert_input,
    routes,
    gate_weights,
    gate_matrix,
    up_matrix,
    down_matrix,
):
    dev_rows, route_count = routes.shape
    width = expert_input.shape[1]
    steps, pairs, heads = lax.axis_size("dp"), lax.axis_size("pair"), lax.axis_size("head")
    sources = steps * pairs
    capacity = max(2, dev_rows * route_count // sources)
    pieces = 8 // capacity

    my_pair, routes = lax.optimization_barrier((my_place("pair", 10**10), routes))
    labels = jnp.pad(routes, ((0, 0), (0, LANES - route_count))).astype(BF16)
    block = jnp.concatenate([expert_input, labels], axis=1)

    def exchange(rows, step):
        return lax.ppermute(rows, "dp", [(i, i ^ step) for i in range(steps)])

    def other_core(rows):
        return lax.ppermute(rows, "pair", [(i, i ^ 1) for i in range(pairs)])

    even = sorted(range(2, steps, 2), reverse=True)
    place = (my_place("dp", 2 * 10**10), my_pair)
    farthest = exchange(block, even[0])
    beside = exchange(block, 1)
    both = jnp.concatenate([block, beside], axis=0)
    mine = [block, beside, farthest] + [exchange(both, step) for step in even[1:]] + [exchange(farthest, 1)]
    order = [0, 1, even[0]] + [s ^ odd for s in even[1:] for odd in (0, 1)] + [even[0] ^ 1]

    attention, lhs = attend(
        lengths, queries, key_cache, value_cache, new_key, new_value, routes, gate_weights,
        capacity, heads, sources,
    )
    sent = expert_block(
        place, mine + [other_core(rows) for rows in mine],
        gate_matrix, up_matrix,
        down_matrix, order, capacity, heads, route_count, dev_rows,
    )
    got = lax.all_to_all(sent, ("dp", "pair", "head"), split_axis=0, concat_axis=0, tiled=True)

    expert_output = pl.pallas_call(
        functools.partial(combine_kernel, pieces, 3),
        out_shape=jax.ShapeDtypeStruct((dev_rows, width // heads), BF16),
        compiler_params=pltpu.CompilerParams(vmem_limit_bytes=8 * 1024 * 1024),
    )(lhs, got)
    return (attention, expert_output)


def solution(mesh):
    placed = (
        P(("groups", "dp", "pair"), "head", None),
        P(("groups", "dp", "pair"), "head", None, None),
        P(("groups", "dp", "pair"), "head", None, None),
        P(("groups", "dp", "pair"), "head", None),
        P(("groups", "dp", "pair"), "head", None),
        P(("groups", "dp", "pair")),
        P(("groups", "dp", "pair"), None),
        P(("groups", "dp", "pair"), None),
        P(("groups", "dp", "pair"), None),
        P(("dp", "pair"), "head", None),
        P(("dp", "pair"), "head", None),
        P(("dp", "pair"), "head", None),
    )
    return jax.shard_map(
        body,
        mesh=mesh,
        in_specs=placed,
        out_specs=(P(("groups", "dp", "pair"), "head", None), P(("groups", "dp", "pair"), "head")),
        check_vma=False,
    )
```
